512 devices in a mesh: ctx: 32 (over x, y, core), ch: 16 (over z).
Axes of the slice: x: 4, y: 4, z: 16, core: 2. Of those that a mesh axis runs over, the one named last changes fastest.
Arguments:
- outer_gate: bfloat16 [16, 524288], P(None, ('ctx', 'ch')), may hold values from -6 to 6
- inner_gate: bfloat16 [16, 524288], P(None, ('ctx', 'ch')), may hold values from -6 to 6
- signal: bfloat16 [16, 524288], P(None, ('ctx', 'ch')), may hold values from -6 to 6
- filter_taps: bfloat16 [16, 524288], P(None, ('ctx', 'ch')), may hold values from -1.5 to 1.5
- skip_gain: float32 [16], replicated, may hold values from -3 to 3
Outputs:
- gated: bfloat16 [16, 524288], P(None, ('ctx', 'ch'))
The draws below stay inside these ranges and needn't reach their ends.
All inputs are finite; a program needn't handle non-finite values.
Results may differ from the reference program's by a relative error of at most 0.012.
Values may be sent and summed in bfloat16 or wider, within the bound.
A program may use at most 64 MiB of HBM per device.

```python
import math
import jax
import jax.numpy as jnp
from jax import lax

SEQUENCE_TOKENS = 524288
WINDOW_CHANNELS = 16


def draw_filter_taps(key, part):
    key = jax.random.fold_in(key, 11)
    falloff_random_key, quick_random_key, jitter_random_key, spike_random_key = jax.random.split(key, 4)
    token_offsets = jnp.arange(SEQUENCE_TOKENS, dtype=jnp.float32)[None, :]
    slow_rate = jnp.exp(jax.random.uniform(falloff_random_key, (WINDOW_CHANNELS, 1), minval=math.log(0.05), maxval=math.log(2.0))) / SEQUENCE_TOKENS
    fast_flag = jax.random.randint(quick_random_key, (WINDOW_CHANNELS, 1), 0, 4) == 0
    fast_rate = 1.0 / jax.random.uniform(jax.random.fold_in(quick_random_key, 1), (WINDOW_CHANNELS, 1), minval=30.0, maxval=50.0)
    falloff_speed = jnp.where(fast_flag, fast_rate, slow_rate)
    coarse_jitter = jnp.clip(jax.random.normal(jitter_random_key, (WINDOW_CHANNELS, SEQUENCE_TOKENS)), -5.0, 5.0)
    spike_locations = jax.random.randint(spike_random_key, (WINDOW_CHANNELS, 3), 0, SEQUENCE_TOKENS).astype(jnp.float32)
    spike_count = jnp.zeros((WINDOW_CHANNELS, SEQUENCE_TOKENS), jnp.float32)
    for column_vector in range(3):
        spike_count = spike_count + (token_offsets >= spike_locations[:, column_vector:column_vector + 1]).astype(jnp.float32)
    kernel_entries = jnp.sqrt(2.0 * falloff_speed) * coarse_jitter * jnp.exp(-falloff_speed * token_offsets + spike_count * math.log(0.6))
    return kernel_entries.astype(jnp.bfloat16)


def levels(own_key, dims, cuts, smallest, high):
    def one(axis_at, shards_of):
        heights = jax.random.uniform(jax.random.fold_in(jax.random.fold_in(own_key, 6), axis_at), (shards_of,), jnp.float32, smallest / len(cuts), high / len(cuts))
        return jnp.repeat(jnp.exp(heights), dims[axis_at] // shards_of).reshape((-1,) + (1,) * (len(dims) - axis_at - 1))

    gain = one(*cuts[0])
    for cut in cuts[1:]:
        gain = gain * one(*cut)
    return gain


def normal_values(own_key, shape, deviation, limit, shards=(), kind=jnp.bfloat16):
    gain = levels(own_key, shape, shards, -0.22, 0.18) if shards else 1.0
    entries = jax.random.normal(own_key, shape, jnp.float32) * deviation * gain
    return jnp.minimum(jnp.maximum(entries, -limit), limit).astype(kind)


def setup_inputs(seed: int = 0) -> dict:
    arg_keys = jax.random.split(jax.random.key(seed), 6)
    outer_gate = normal_values(arg_keys[0], (WINDOW_CHANNELS, SEQUENCE_TOKENS), 1.0, 6.0, ((1, 512),))
    inner_gate = normal_values(arg_keys[1], (WINDOW_CHANNELS, SEQUENCE_TOKENS), 1.0, 6.0, ((1, 512),))
    signal = normal_values(arg_keys[2], (WINDOW_CHANNELS, SEQUENCE_TOKENS), 1.0, 6.0, ((1, 512),))
    filter_taps = draw_filter_taps(jax.random.fold_in(arg_keys[5], 71), 0)
    skip_gain = normal_values(arg_keys[4], (WINDOW_CHANNELS,), 1.0, 3.0, (), jnp.float32)
    return dict(outer_gate=outer_gate, inner_gate=inner_gate, signal=signal, filter_taps=filter_taps, skip_gain=skip_gain)


def channel_conv(pair_rows):
    input_row, taps_row = pair_rows
    length = input_row.shape[-1]
    product = jnp.fft.rfft(input_row, n=2 * length) * jnp.fft.rfft(taps_row, n=2 * length)
    return jnp.fft.irfft(product, n=2 * length)[:length]


def reference(outer_gate, inner_gate, signal, filter_taps, skip_gain):
    mixed_input = (inner_gate.astype(jnp.float32) * signal.astype(jnp.float32)).astype(jnp.bfloat16)
    conv_out = lax.map(channel_conv, (mixed_input.astype(jnp.float32), filter_taps.astype(jnp.float32)))
    conv_out = conv_out.astype(jnp.float32).astype(jnp.bfloat16)
    total = conv_out.astype(jnp.float32) + skip_gain[:, None] * mixed_input.astype(jnp.float32)
    return (outer_gate.astype(jnp.float32) * total).astype(jnp.bfloat16)
```

```python
import functools
import math

import jax
import jax.numpy as jnp
import ml_dtypes
import numpy as np
from jax import lax
from jax.experimental import pallas as pl
from jax.experimental.pallas import tpu as pltpu
from jax.sharding import PartitionSpec as P

MESH = pl.DeviceIdType.MESH
LANES = 128
ROWS = 8


def split_bf16(table):
    high = table.astype(ml_dtypes.bfloat16)
    low = (table - high.astype(np.float64)).astype(ml_dtypes.bfloat16)
    return np.stack([high, low])


def make_tables(planes, blocks):
    units = ROWS * planes
    length = units * LANES
    part = units // blocks
    block, kind, row = np.meshgrid(np.arange(blocks), np.arange(2), np.arange(part), indexing="ij")
    row_first = (block * part + row).reshape(-1)
    row_kind = kind.reshape(-1)
    plane, column_kind, sub = np.meshgrid(np.arange(planes), np.arange(2), np.arange(ROWS), indexing="ij")
    unit = (plane * ROWS + sub).reshape(-1)
    column_kind = column_kind.reshape(-1)
    lane = np.arange(LANES)

    angle = 0.5 * np.pi * LANES * unit[None, :] / length
    angle = angle - 2 * np.pi * ((row_first[:, None] * unit[None, :]) % units) / units
    same = row_kind[:, None] == column_kind[None, :]
    first = np.concatenate([np.cos(angle) * same, np.sin(angle) * same])

    angle = 0.5 * np.pi * lane[None, :] / length - 2 * np.pi * row_first[:, None] * lane[None, :] / length
    twist = np.stack([np.cos(angle), np.sin(angle)])

    angle = 2 * np.pi * ((lane[:, None] * lane[None, :]) % LANES) / LANES
    cosine, sine = np.cos(angle), np.sin(angle)
    second = np.block([[cosine, -sine], [sine, cosine]])
    back = np.concatenate([cosine, sine], axis=1)

    real, imag = twist[0], -twist[1]
    is_real = row_kind[:, None] == 0
    untwist = np.stack([np.where(is_real, real, -imag), np.where(is_real, -imag, -real)])

    every_unit = np.arange(units)
    angle = -0.5 * np.pi * LANES * every_unit[:, None] / length
    angle = angle + 2 * np.pi * ((every_unit[:, None] * row_first[None, :]) % units) / units
    last = np.concatenate([np.cos(angle), -np.sin(angle)], axis=1) / length
    return (
        split_bf16(first),
        twist.astype(np.float32),
        split_bf16(second),
        split_bf16(back),
        untwist.astype(np.float32),
        split_bf16(last),
    )


def dot(left, right):
    return jnp.dot(left, right, preferred_element_type=jnp.float32)


def halves(value):
    high = value.astype(jnp.bfloat16)
    low = (value - high.astype(jnp.float32)).astype(jnp.bfloat16)
    return high, low


def kernel(planes, blocks, inner_hbm, signal_hbm, taps_hbm, outer_hbm, skip_ref, first_hbm, twist_hbm,
           second_hbm, back_hbm, untwist_hbm, last_hbm, out_ref,
           inner, signal, taps, outer, first, twist, second, back, untwist, last,
           mixed, staged, send1, recv1, send2, recv2, xa, xb, ha, hb, send3, recv3, send4, recv4,
           load_sem, send_sem, recv_sem):
    me = lax.axis_index("ctx")
    plane = lax.axis_index("ch")
    channels = planes
    units = ROWS * planes
    part = units // blocks

    barrier = pltpu.get_barrier_semaphore()
    for k in range(1, planes):
        pl.semaphore_signal(barrier, inc=1, device_id=(me, (plane + k) % planes), device_id_type=MESH)
    for k in range(1, blocks):
        pl.semaphore_signal(barrier, inc=1, device_id=((me + k) % blocks, plane), device_id_type=MESH)

    sources = (inner_hbm, signal_hbm, taps_hbm, outer_hbm, first_hbm, twist_hbm, second_hbm, back_hbm,
               untwist_hbm, last_hbm)
    places = (inner, signal, taps, outer, first, twist, second, back, untwist, last)
    loads = [pltpu.make_async_copy(s, d, load_sem.at[i]) for i, (s, d) in enumerate(zip(sources, places))]
    for load in loads:
        load.start()
    for load in loads[:3]:
        load.wait()

    product = inner[...].astype(jnp.float32) * signal[...].astype(jnp.float32)
    product = product.astype(jnp.bfloat16).astype(jnp.float32)
    mixed[...] = product
    filters = taps[...].astype(jnp.float32)
    for s in range(ROWS):
        columns = slice(s * LANES, (s + 1) * LANES)
        staged[pl.ds(s, channels, stride=2 * ROWS), :] = product[:, columns]
        staged[pl.ds(ROWS + s, channels, stride=2 * ROWS), :] = filters[:, columns]
    send1[...] = staged[...].reshape(channels, 2 * ROWS, LANES).astype(jnp.bfloat16)
    recv1[plane] = send1[plane]

    pl.semaphore_wait(barrier, planes + blocks - 2)

    def landing(target, slot):
        if target is recv4:
            return recv4.at[pl.ds(pl.multiple_of(slot * ROWS, ROWS), ROWS)]
        return target.at[slot]

    def exchange(stage, source, target, over_planes):
        size, here = (planes, plane) if over_planes else (blocks, me)
        for k in range(1, size):
            there = (here + k) % size
            pltpu.make_async_remote_copy(
                src_ref=source.at[there],
                dst_ref=landing(target, here),
                send_sem=send_sem.at[stage],
                recv_sem=recv_sem.at[stage],
                device_id=(me, there) if over_planes else (there, plane),
                device_id_type=MESH,
            ).start()

    def whole(stage, source, target):
        size = source.shape[0]
        return pltpu.make_async_remote_copy(
            src_ref=source.at[pl.ds(0, size - 1)],
            dst_ref=target.at[pl.ds(0, (size - 1) * (target.shape[0] // size))],
            send_sem=send_sem.at[stage],
            recv_sem=recv_sem.at[stage],
            device_id=(me, plane),
            device_id_type=MESH,
        )

    exchange(0, send1, recv1, True)
    for load in loads[3:]:
        load.wait()
    whole(0, send1, recv1).wait_recv()

    values = recv1[...].reshape(2 * units, LANES)
    along = dot(first[0], values) + dot(first[1], values)
    real, imag = along[: 2 * units], along[2 * units :]
    turned = jnp.concatenate(
        [real * twist[0] - imag * twist[1], real * twist[1] + imag * twist[0]], axis=1
    )
    high, low = halves(turned)
    spectrum = dot(high, second[0]) + dot(low, second[0]) + dot(high, second[1])
    send2[...] = jnp.concatenate(
        [
            spectrum[:, :LANES].reshape(blocks, ROWS, LANES),
            spectrum[:, LANES:].reshape(blocks, ROWS, LANES),
        ],
        axis=1,
    ).astype(jnp.bfloat16)
    recv2[me] = send2[me]
    exchange(1, send2, recv2, False)
    whole(1, send2, recv2).wait_recv()

    pieces = recv2[...].astype(jnp.float32)
    upper = lax.broadcasted_iota(jnp.int32, (blocks, ROWS, LANES), 1) < part
    real, imag = pieces[:, :ROWS], pieces[:, ROWS:]
    real_rolled = jnp.roll(real, part, axis=1)
    imag_rolled = jnp.roll(imag, part, axis=1)
    xa[...] = jnp.where(upper, real, imag_rolled)
    xb[...] = jnp.where(upper, imag, real_rolled)
    ha[...] = jnp.where(upper, real_rolled, real)
    hb[...] = jnp.where(upper, -imag_rolled, imag)
    sign = jnp.where(lax.broadcasted_iota(jnp.int32, (ROWS, LANES), 0) < part, 1.0, -1.0)
    group = min(8, blocks)
    before = jnp.zeros((ROWS, LANES), jnp.float32)
    for start in range(0, blocks, group):
        sums = [jnp.zeros((ROWS, LANES), jnp.float32) for _ in range(group)]
        for i in range(start + group):
            x_direct, x_crossed = xa[i], xb[i]
            for offset in range(group):
                j = start + offset - i
                if j >= 0:
                    sums[offset] = sums[offset] + (x_direct * ha[j] + x_crossed * hb[j])
        for offset in range(group):
            send3[start + offset] = sums[offset] + sign * jnp.roll(before, part, axis=0)
            before = sums[offset]
    recv3[me] = send3[me]
    exchange(2, send3, recv3, False)
    whole(2, send3, recv3).wait_recv()

    high, low = halves(recv3[...].reshape(2 * units, LANES))
    lanes_back = dot(high, back[0]) + dot(low, back[0]) + dot(high, back[1])
    first_half, second_half = lanes_back[:, :LANES], lanes_back[:, LANES:]
    turned = jnp.concatenate(
        [
            first_half * untwist[0] + second_half * untwist[1],
            second_half * untwist[0] - first_half * untwist[1],
        ],
        axis=0,
    )
    high, low = halves(turned)
    result = dot(last[0], high) + dot(last[0], low) + dot(last[1], high)
    send4[...] = result.reshape(planes, ROWS, LANES)
    landing(recv4, plane)[...] = send4[plane]
    exchange(3, send4, recv4, True)

    channel = lax.broadcasted_iota(jnp.int32, (channels, LANES), 0)
    skip = jnp.zeros((channels, LANES), jnp.float32)
    for c in range(channels):
        skip = jnp.where(channel == c, skip_ref[c], skip)
    whole(3, send4, recv4).wait_recv()

    for s in range(ROWS):
        columns = slice(s * LANES, (s + 1) * LANES)
        conv = recv4[pl.ds(s, channels, stride=ROWS), :].astype(jnp.bfloat16).astype(jnp.float32)
        total = conv + skip * mixed[:, columns]
        out_ref[:, columns] = (outer[:, columns].astype(jnp.float32) * total).astype(jnp.bfloat16)

    whole(0, send1, recv1).wait_send()
    whole(1, send2, recv2).wait_send()
    whole(2, send3, recv3).wait_send()
    whole(3, send4, recv4).wait_send()


def local(planes, blocks, outer_gate, inner_gate, signal, filter_taps, skip_gain):
    channels, tokens = signal.shape
    tables = make_tables(planes, blocks)
    anywhere = pl.BlockSpec(memory_space=pl.ANY)
    bf16, f32 = jnp.bfloat16, jnp.float32
    tile = (ROWS, LANES)
    scratch = [pltpu.VMEM((channels, tokens), bf16)] * 4
    scratch += [pltpu.VMEM(t.shape, t.dtype) for t in tables]
    scratch += [
        pltpu.VMEM((channels, tokens), f32),
        pltpu.VMEM((channels * 2 * ROWS, LANES), f32),
        pltpu.VMEM((channels, 2 * ROWS, LANES), bf16),
        pltpu.VMEM((planes, 2 * ROWS, LANES), bf16),
        pltpu.VMEM((blocks, 2 * ROWS, LANES), bf16),
        pltpu.VMEM((blocks, 2 * ROWS, LANES), bf16),
    ]
    scratch += [pltpu.VMEM((blocks,) + tile, f32)] * 6
    scratch += [pltpu.VMEM((planes,) + tile, f32)]
    scratch += [pltpu.VMEM((planes * ROWS, LANES), f32)]
    scratch += [
        pltpu.SemaphoreType.DMA((10,)),
        pltpu.SemaphoreType.DMA((4,)),
        pltpu.SemaphoreType.DMA((4,)),
    ]
    return pl.pallas_call(
        functools.partial(kernel, planes, blocks),
        out_shape=jax.ShapeDtypeStruct((channels, tokens), bf16),
        in_specs=[anywhere] * 4 + [pl.BlockSpec(memory_space=pltpu.SMEM)] + [anywhere] * 6,
        out_specs=pl.BlockSpec(memory_space=pltpu.VMEM),
        scratch_shapes=scratch,
        compiler_params=pltpu.CompilerParams(collective_id=0, has_side_effects=True),
        name="hyena_conv",
    )(inner_gate, signal, filter_taps, outer_gate, skip_gain, *[jnp.asarray(t) for t in tables])


def solution(mesh):
    spec = P(None, ("ctx", "ch"))
    return jax.shard_map(
        functools.partial(local, mesh.shape["ch"], mesh.shape["ctx"]),
        mesh=mesh,
        in_specs=(spec, spec, spec, spec, P()),
        out_specs=spec,
        check_vma=False,
    )
```

```python
import functools
import math

import jax
import jax.numpy as jnp
import ml_dtypes
import numpy as np
from jax import lax
from jax.experimental import pallas as pl
from jax.experimental.pallas import tpu as pltpu
from jax.sharding import PartitionSpec as P

MESH = pl.DeviceIdType.MESH
LANES = 128
ROWS = 8


def split_bf16(table):
    high = table.astype(ml_dtypes.bfloat16)
    low = (table - high.astype(np.float64)).astype(ml_dtypes.bfloat16)
    return np.stack([high, low])


def make_tables(planes, blocks):
    units = ROWS * planes
    length = units * LANES
    part = units // blocks
    block, kind, row = np.meshgrid(np.arange(blocks), np.arange(2), np.arange(part), indexing="ij")
    row_first = (block * part + row).reshape(-1)
    row_kind = kind.reshape(-1)
    plane, column_kind, sub = np.meshgrid(np.arange(planes), np.arange(2), np.arange(ROWS), indexing="ij")
    unit = (plane * ROWS + sub).reshape(-1)
    column_kind = column_kind.reshape(-1)
    lane = np.arange(LANES)

    angle = 0.5 * np.pi * LANES * unit[None, :] / length
    angle = angle - 2 * np.pi * ((row_first[:, None] * unit[None, :]) % units) / units
    same = row_kind[:, None] == column_kind[None, :]
    first = np.concatenate([np.cos(angle) * same, np.sin(angle) * same])

    angle = 0.5 * np.pi * lane[None, :] / length - 2 * np.pi * row_first[:, None] * lane[None, :] / length
    twist = np.stack([np.cos(angle), np.sin(angle)])

    angle = 2 * np.pi * ((lane[:, None] * lane[None, :]) % LANES) / LANES
    cosine, sine = np.cos(angle), np.sin(angle)
    second = np.block([[cosine, -sine], [sine, cosine]])
    back = np.concatenate([cosine, sine], axis=1)

    real, imag = twist[0], -twist[1]
    is_real = row_kind[:, None] == 0
    untwist = np.stack([np.where(is_real, real, -imag), np.where(is_real, -imag, -real)])

    every_unit = np.arange(units)
    angle = -0.5 * np.pi * LANES * every_unit[:, None] / length
    angle = angle + 2 * np.pi * ((every_unit[:, None] * row_first[None, :]) % units) / units
    last = np.concatenate([np.cos(angle), -np.sin(angle)], axis=1) / length
    return (
        split_bf16(first),
        twist.astype(np.float32),
        split_bf16(second),
        split_bf16(back),
        untwist.astype(np.float32),
        split_bf16(last),
    )


def dot(left, right):
    return jnp.dot(left, right, preferred_element_type=jnp.float32)


def halves(value):
    high = value.astype(jnp.bfloat16)
    low = (value - high.astype(jnp.float32)).astype(jnp.bfloat16)
    return high, low


def far_first(size, ring):
    def around(k, n):
        return min(k, n - k)

    def distance(k):
        if ring:
            return around(k, size)
        side = max(1, math.isqrt(size // 2))
        return around(k // (2 * side), side) + around(k // 2 % side, side)

    return sorted(range(1, size), key=lambda k: -distance(k))


def kernel(planes, blocks, inner_hbm, signal_hbm, taps_hbm, outer_hbm, skip_ref, first_hbm, twist_hbm,
           second_hbm, back_hbm, untwist_hbm, last_hbm, out_ref,
           inner, signal, taps, outer, first, twist, second, back, untwist, last,
           mixed, staged, send1, recv1, send2, recv2, xa, xb, ha, hb, send3, recv3, send4, recv4,
           load_sem, send_sem, recv_sem):
    me = lax.axis_index("ctx")
    plane = lax.axis_index("ch")
    channels = planes
    units = ROWS * planes
    part = units // blocks

    barrier = pltpu.get_barrier_semaphore()
    for k in range(1, planes):
        pl.semaphore_signal(barrier, inc=1, device_id=(me, (plane + k) % planes), device_id_type=MESH)
    for k in range(1, blocks):
        pl.semaphore_signal(barrier, inc=1, device_id=((me + k) % blocks, plane), device_id_type=MESH)

    sources = (inner_hbm, signal_hbm, taps_hbm, outer_hbm, first_hbm, twist_hbm, second_hbm, back_hbm,
               untwist_hbm, last_hbm)
    places = (inner, signal, taps, outer, first, twist, second, back, untwist, last)
    loads = [pltpu.make_async_copy(s, d, load_sem.at[i]) for i, (s, d) in enumerate(zip(sources, places))]
    for load in loads:
        load.start()
    for load in loads[:3]:
        load.wait()

    product = inner[...].astype(jnp.float32) * signal[...].astype(jnp.float32)
    product = product.astype(jnp.bfloat16).astype(jnp.float32)
    mixed[...] = product
    filters = taps[...].astype(jnp.float32)
    for s in range(ROWS):
        columns = slice(s * LANES, (s + 1) * LANES)
        staged[pl.ds(s, channels, stride=2 * ROWS), :] = product[:, columns]
        staged[pl.ds(ROWS + s, channels, stride=2 * ROWS), :] = filters[:, columns]
    send1[...] = staged[...].reshape(channels, 2 * ROWS, LANES).astype(jnp.bfloat16)
    recv1[plane] = send1[plane]

    pl.semaphore_wait(barrier, planes + blocks - 2)

    def landing(target, slot):
        if target is recv4:
            return recv4.at[pl.ds(pl.multiple_of(slot * ROWS, ROWS), ROWS)]
        return target.at[slot]

    def exchange(stage, source, target, over_planes):
        size, here = (planes, plane) if over_planes else (blocks, me)
        for k in far_first(size, over_planes):
            there = (here + k) % size
            pltpu.make_async_remote_copy(
                src_ref=source.at[there],
                dst_ref=landing(target, here),
                send_sem=send_sem.at[stage],
                recv_sem=recv_sem.at[stage],
                device_id=(me, there) if over_planes else (there, plane),
                device_id_type=MESH,
            ).start()

    def whole(stage, source, target):
        size = source.shape[0]
        return pltpu.make_async_remote_copy(
            src_ref=source.at[pl.ds(0, size - 1)],
            dst_ref=target.at[pl.ds(0, (size - 1) * (target.shape[0] // size))],
            send_sem=send_sem.at[stage],
            recv_sem=recv_sem.at[stage],
            device_id=(me, plane),
            device_id_type=MESH,
        )

    exchange(0, send1, recv1, True)
    for load in loads[3:]:
        load.wait()
    whole(0, send1, recv1).wait_recv()

    values = recv1[...].reshape(2 * units, LANES)
    along = dot(first[0], values) + dot(first[1], values)
    real, imag = along[: 2 * units], along[2 * units :]
    turned = jnp.concatenate(
        [real * twist[0] - imag * twist[1], real * twist[1] + imag * twist[0]], axis=1
    )
    high, low = halves(turned)
    spectrum = dot(high, second[0]) + dot(low, second[0]) + dot(high, second[1])
    send2[...] = jnp.concatenate(
        [
            spectrum[:, :LANES].reshape(blocks, ROWS, LANES),
            spectrum[:, LANES:].reshape(blocks, ROWS, LANES),
        ],
        axis=1,
    ).astype(jnp.bfloat16)
    recv2[me] = send2[me]
    exchange(1, send2, recv2, False)
    whole(1, send2, recv2).wait_recv()

    pieces = recv2[...].astype(jnp.float32)
    upper = lax.broadcasted_iota(jnp.int32, (blocks, ROWS, LANES), 1) < part
    real, imag = pieces[:, :ROWS], pieces[:, ROWS:]
    real_rolled = jnp.roll(real, part, axis=1)
    imag_rolled = jnp.roll(imag, part, axis=1)
    xa[...] = jnp.where(upper, real, imag_rolled)
    xb[...] = jnp.where(upper, imag, real_rolled)
    ha[...] = jnp.where(upper, real_rolled, real)
    hb[...] = jnp.where(upper, -imag_rolled, imag)
    sign = jnp.where(lax.broadcasted_iota(jnp.int32, (ROWS, LANES), 0) < part, 1.0, -1.0)
    group = min(8, blocks)
    before = jnp.zeros((ROWS, LANES), jnp.float32)
    for start in range(0, blocks, group):
        sums = [jnp.zeros((ROWS, LANES), jnp.float32) for _ in range(group)]
        for i in range(start + group):
            x_direct, x_crossed = xa[i], xb[i]
            for offset in range(group):
                j = start + offset - i
                if j >= 0:
                    sums[offset] = sums[offset] + (x_direct * ha[j] + x_crossed * hb[j])
        for offset in range(group):
            send3[start + offset] = sums[offset] + sign * jnp.roll(before, part, axis=0)
            before = sums[offset]
    recv3[me] = send3[me]
    exchange(2, send3, recv3, False)
    whole(2, send3, recv3).wait_recv()

    high, low = halves(recv3[...].reshape(2 * units, LANES))
    lanes_back = dot(high, back[0]) + dot(low, back[0]) + dot(high, back[1])
    first_half, second_half = lanes_back[:, :LANES], lanes_back[:, LANES:]
    turned = jnp.concatenate(
        [
            first_half * untwist[0] + second_half * untwist[1],
            second_half * untwist[0] - first_half * untwist[1],
        ],
        axis=0,
    )
    high, low = halves(turned)
    result = dot(last[0], high) + dot(last[0], low) + dot(last[1], high)
    send4[...] = result.reshape(planes, ROWS, LANES)
    landing(recv4, plane)[...] = send4[plane]
    exchange(3, send4, recv4, True)

    channel = lax.broadcasted_iota(jnp.int32, (channels, LANES), 0)
    skip = jnp.zeros((channels, LANES), jnp.float32)
    for c in range(channels):
        skip = jnp.where(channel == c, skip_ref[c], skip)
    whole(3, send4, recv4).wait_recv()

    for s in range(ROWS):
        columns = slice(s * LANES, (s + 1) * LANES)
        conv = recv4[pl.ds(s, channels, stride=ROWS), :].astype(jnp.bfloat16).astype(jnp.float32)
        total = conv + skip * mixed[:, columns]
        out_ref[:, columns] = (outer[:, columns].astype(jnp.float32) * total).astype(jnp.bfloat16)

    whole(0, send1, recv1).wait_send()
    whole(1, send2, recv2).wait_send()
    whole(2, send3, recv3).wait_send()
    whole(3, send4, recv4).wait_send()


def local(planes, blocks, outer_gate, inner_gate, signal, filter_taps, skip_gain):
    channels, tokens = signal.shape
    tables = make_tables(planes, blocks)
    anywhere = pl.BlockSpec(memory_space=pl.ANY)
    bf16, f32 = jnp.bfloat16, jnp.float32
    tile = (ROWS, LANES)
    scratch = [pltpu.VMEM((channels, tokens), bf16)] * 4
    scratch += [pltpu.VMEM(t.shape, t.dtype) for t in tables]
    scratch += [
        pltpu.VMEM((channels, tokens), f32),
        pltpu.VMEM((channels * 2 * ROWS, LANES), f32),
        pltpu.VMEM((channels, 2 * ROWS, LANES), bf16),
        pltpu.VMEM((planes, 2 * ROWS, LANES), bf16),
        pltpu.VMEM((blocks, 2 * ROWS, LANES), bf16),
        pltpu.VMEM((blocks, 2 * ROWS, LANES), bf16),
    ]
    scratch += [pltpu.VMEM((blocks,) + tile, f32)] * 6
    scratch += [pltpu.VMEM((planes,) + tile, f32)]
    scratch += [pltpu.VMEM((planes * ROWS, LANES), f32)]
    scratch += [
        pltpu.SemaphoreType.DMA((10,)),
        pltpu.SemaphoreType.DMA((4,)),
        pltpu.SemaphoreType.DMA((4,)),
    ]
    return pl.pallas_call(
        functools.partial(kernel, planes, blocks),
        out_shape=jax.ShapeDtypeStruct((channels, tokens), bf16),
        in_specs=[anywhere] * 4 + [pl.BlockSpec(memory_space=pltpu.SMEM)] + [anywhere] * 6,
        out_specs=pl.BlockSpec(memory_space=pltpu.VMEM),
        scratch_shapes=scratch,
        compiler_params=pltpu.CompilerParams(collective_id=0, has_side_effects=True),
        name="hyena_conv",
    )(inner_gate, signal, filter_taps, outer_gate, skip_gain, *[jnp.asarray(t) for t in tables])


def solution(mesh):
    spec = P(None, ("ctx", "ch"))
    return jax.shard_map(
        functools.partial(local, mesh.shape["ch"], mesh.shape["ctx"]),
        mesh=mesh,
        in_specs=(spec, spec, spec, spec, P()),
        out_specs=spec,
        check_vma=False,
    )
```

```python
import functools
import math

import jax
import jax.numpy as jnp
import ml_dtypes
import numpy as np
from jax import lax
from jax.experimental import pallas as pl
from jax.experimental.pallas import tpu as pltpu
from jax.sharding import PartitionSpec as P

MESH = pl.DeviceIdType.MESH
LANES = 128
ROWS = 8
PAIR = 2
SHIFT = 1


def split_bf16(table):
    high = table.astype(ml_dtypes.bfloat16)
    low = (table - high.astype(np.float64)).astype(ml_dtypes.bfloat16)
    return np.stack([high, low])


def make_tables(planes, blocks):
    units = ROWS * planes
    length = units * LANES
    part = units // blocks
    block, kind, row = np.meshgrid(np.arange(blocks), np.arange(2), np.arange(part), indexing="ij")
    row_first = (block * part + row).reshape(-1)
    row_kind = kind.reshape(-1)
    plane, column_kind, sub = np.meshgrid(np.arange(planes), np.arange(2), np.arange(ROWS), indexing="ij")
    unit = (plane * ROWS + sub).reshape(-1)
    column_kind = column_kind.reshape(-1)
    lane = np.arange(LANES)

    angle = 0.5 * np.pi * LANES * unit[None, :] / length
    angle = angle - 2 * np.pi * ((row_first[:, None] * unit[None, :]) % units) / units
    same = row_kind[:, None] == column_kind[None, :]
    first = np.concatenate([np.cos(angle) * same, np.sin(angle) * same])

    angle = 0.5 * np.pi * lane[None, :] / length - 2 * np.pi * row_first[:, None] * lane[None, :] / length
    twist = np.stack([np.cos(angle), np.sin(angle)])

    angle = 2 * np.pi * ((lane[:, None] * lane[None, :]) % LANES) / LANES
    cosine, sine = np.cos(angle), np.sin(angle)
    second = np.block([[cosine, -sine], [sine, cosine]])
    back = np.concatenate([cosine, sine], axis=1)

    real, imag = twist[0], -twist[1]
    is_real = row_kind[:, None] == 0
    untwist = np.stack([np.where(is_real, real, -imag), np.where(is_real, -imag, -real)])

    every_unit = np.arange(units)
    angle = -0.5 * np.pi * LANES * every_unit[:, None] / length
    angle = angle + 2 * np.pi * ((every_unit[:, None] * row_first[None, :]) % units) / units
    last = np.concatenate([np.cos(angle), -np.sin(angle)], axis=1) / length
    return (
        split_bf16(first),
        twist.astype(np.float32),
        split_bf16(second),
        split_bf16(back),
        untwist.astype(np.float32),
        split_bf16(last),
    )


def dot(left, right):
    return jnp.dot(left, right, preferred_element_type=jnp.float32)


def halves(value):
    high = value.astype(jnp.bfloat16)
    low = (value - high.astype(jnp.float32)).astype(jnp.bfloat16)
    return high, low


def far_first(size, ring):
    def around(k, n):
        return min(k, n - k)

    def distance(k):
        if ring:
            return around(k, size)
        side = max(1, math.isqrt(size // 2))
        return around(k // (2 * side), side) + around(k // 2 % side, side)

    return sorted(range(1, size), key=lambda k: -distance(k))


def kernel(planes, blocks, inner_hbm, signal_hbm, taps_hbm, outer_hbm, skip_hbm, first_hbm, twist_hbm,
           second_hbm, back_hbm, untwist_hbm, last_hbm, out_ref,
           inner, signal, taps, outer, skip_scalars, first, twist, second, back, untwist, last,
           mixed, staged, send1, recv1, send2, recv2, xa, xb, ha, hb, product, send3, recv3, send4, recv4, rows4,
           load_sem, send_sem, recv_sem):
    me = lax.axis_index("ctx")
    plane = lax.axis_index("ch")
    channels = planes
    owners = planes // PAIR

    def rank(z):
        return (z + SHIFT) % planes

    units = ROWS * planes
    part = units // blocks
    is_owner = rank(plane) < owners
    mine = rank(plane)
    ring = far_first(planes, True)
    flat = far_first(blocks, False)

    barrier = pltpu.get_barrier_semaphore()

    @pl.when(is_owner)
    def _():
        for k in ring:
            pl.semaphore_signal(barrier, inc=1, device_id=(me, (plane + k) % planes), device_id_type=MESH)
        for k in flat:
            pl.semaphore_signal(barrier, inc=1, device_id=((me + k) % blocks, plane), device_id_type=MESH)

    sources = (inner_hbm, signal_hbm, taps_hbm, outer_hbm, skip_hbm, first_hbm, twist_hbm, second_hbm,
               back_hbm, untwist_hbm, last_hbm)
    places = (inner, signal, taps, outer, skip_scalars, first, twist, second, back, untwist, last)
    loads = [pltpu.make_async_copy(s, d, load_sem.at[i]) for i, (s, d) in enumerate(zip(sources, places))]
    for load in loads[:5]:
        load.start()
    for load in loads[:3]:
        load.wait()

    gated = inner[...].astype(jnp.float32) * signal[...].astype(jnp.float32)
    gated = gated.astype(jnp.bfloat16).astype(jnp.float32)
    mixed[...] = gated
    filters = taps[...].astype(jnp.float32)
    for s in range(ROWS):
        columns = slice(s * LANES, (s + 1) * LANES)
        staged[pl.ds(s, channels, stride=2 * ROWS), :] = gated[:, columns]
        staged[pl.ds(ROWS + s, channels, stride=2 * ROWS), :] = filters[:, columns]
    send1[...] = staged[...].reshape(owners, PAIR * 2 * ROWS, LANES).astype(jnp.bfloat16)

    pl.semaphore_wait(barrier, jnp.where(is_owner, owners + blocks - 2, owners))

    def remote(stage, source, target, device):
        return pltpu.make_async_remote_copy(
            src_ref=source,
            dst_ref=target,
            send_sem=send_sem.at[stage],
            recv_sem=recv_sem.at[stage],
            device_id=device,
            device_id_type=MESH,
        )

    def whole(stage, buffer, slots):
        return remote(stage, buffer.at[pl.ds(0, slots)], buffer.at[pl.ds(0, slots)], (me, plane))

    for k in ring:
        there = (plane + k) % planes

        @pl.when(rank(there) < owners)
        def _(there=there):
            remote(0, send1.at[rank(there)], recv1.at[plane], (me, there)).start()

    @pl.when(is_owner)
    def _():
        for load in loads[5:]:
            load.start()
        recv1[plane] = send1[mine]
        for load in loads[5:]:
            load.wait()
        whole(0, recv1, planes - 1).wait_recv()

        per_channel = 2 * ROWS
        values = jnp.concatenate(
            [
                recv1[:, c * per_channel : (c + 1) * per_channel, :].reshape(2 * units, LANES)
                for c in range(PAIR)
            ],
            axis=1,
        )
        along = dot(first[0], values) + dot(first[1], values)
        for c in range(PAIR):
            real = along[: 2 * units, c * LANES : (c + 1) * LANES]
            imag = along[2 * units :, c * LANES : (c + 1) * LANES]
            turned = jnp.concatenate(
                [real * twist[0] - imag * twist[1], real * twist[1] + imag * twist[0]], axis=1
            )
            high, low = halves(turned)
            spectrum = dot(high, second[0]) + dot(low, second[0]) + dot(high, second[1])
            send2[c] = jnp.concatenate(
                [
                    spectrum[:, :LANES].reshape(blocks, ROWS, LANES),
                    spectrum[:, LANES:].reshape(blocks, ROWS, LANES),
                ],
                axis=1,
            ).astype(jnp.bfloat16)
            recv2[c, me] = send2[c, me]
            for k in flat:
                there = (me + k) % blocks
                remote(1 + c, send2.at[c, there], recv2.at[c, me], (there, plane)).start()

        upper = lax.broadcasted_iota(jnp.int32, (blocks, ROWS, LANES), 1) < part
        sign = jnp.where(lax.broadcasted_iota(jnp.int32, (ROWS, LANES), 0) < part, 1.0, -1.0)
        group = min(8, blocks)
        for c in range(PAIR):
            whole(1 + c, recv2.at[c], blocks - 1).wait_recv()
            pieces = recv2[c].astype(jnp.float32)
            real, imag = pieces[:, :ROWS], pieces[:, ROWS:]
            real_rolled = jnp.roll(real, part, axis=1)
            imag_rolled = jnp.roll(imag, part, axis=1)
            xa[...] = jnp.where(upper, real, imag_rolled)
            xb[...] = jnp.where(upper, imag, real_rolled)
            ha[...] = jnp.where(upper, real_rolled, real)
            hb[...] = jnp.where(upper, -imag_rolled, imag)
            before = jnp.zeros((ROWS, LANES), jnp.float32)
            for start in range(0, blocks, group):
                sums = [jnp.zeros((ROWS, LANES), jnp.float32) for _ in range(group)]
                for i in range(start + group):
                    x_direct, x_crossed = xa[i], xb[i]
                    for offset in range(group):
                        j = start + offset - i
                        if j >= 0:
                            sums[offset] = sums[offset] + (x_direct * ha[j] + x_crossed * hb[j])
                for offset in range(group):
                    product[start + offset, c * ROWS : (c + 1) * ROWS, :] = sums[offset] + sign * jnp.roll(
                        before, part, axis=0
                    )
                    before = sums[offset]
        send3[...] = product[...].astype(jnp.bfloat16)
        recv3[me] = send3[me]
        for k in flat:
            there = (me + k) % blocks
            remote(1 + PAIR, send3.at[there], recv3.at[me], (there, plane)).start()
        whole(1 + PAIR, recv3, blocks - 1).wait_recv()

        waves = recv3[...].reshape(blocks * PAIR * ROWS, LANES)
        lanes_back = (dot(waves, back[0]) + dot(waves, back[1])).reshape(blocks, PAIR, ROWS, 2 * LANES)
        turned = []
        for c in range(PAIR):
            lanes_c = lanes_back[:, c].reshape(2 * units, 2 * LANES)
            first_half, second_half = lanes_c[:, :LANES], lanes_c[:, LANES:]
            turned.append(
                jnp.concatenate(
                    [
                        first_half * untwist[0] + second_half * untwist[1],
                        second_half * untwist[0] - first_half * untwist[1],
                    ],
                    axis=0,
                )
            )
        high, low = halves(jnp.concatenate(turned, axis=1))
        result = dot(last[0], high) + dot(last[0], low) + dot(last[1], high)
        send4[...] = jnp.concatenate(
            [result[:, c * LANES : (c + 1) * LANES].reshape(planes, ROWS, LANES) for c in range(PAIR)], axis=1
        ).astype(jnp.bfloat16)
        recv4[mine] = send4[plane]
        for k in ring:
            there = (plane + k) % planes
            remote(2 + PAIR, send4.at[there], recv4.at[mine], (me, there)).start()

    channel = lax.broadcasted_iota(jnp.int32, (channels, LANES), 0)
    loads[3].wait()
    loads[4].wait()
    skip = jnp.zeros((channels, LANES), jnp.float32)
    for c in range(channels):
        skip = jnp.where(channel == c, skip_scalars[c], skip)

    @pl.when(is_owner)
    def _():
        whole(2 + PAIR, recv4, owners - 1).wait_recv()

    @pl.when(jnp.logical_not(is_owner))
    def _():
        whole(2 + PAIR, recv4, owners).wait_recv()

    rows4[...] = recv4[...].astype(jnp.float32).reshape(channels * ROWS, LANES)
    for s in range(ROWS):
        columns = slice(s * LANES, (s + 1) * LANES)
        conv = rows4[pl.ds(s, channels, stride=ROWS), :]
        total = conv + skip * mixed[:, columns]
        out_ref[:, columns] = (outer[:, columns].astype(jnp.float32) * total).astype(jnp.bfloat16)

    @pl.when(is_owner)
    def _():
        whole(0, send1, owners - 1).wait_send()
        for c in range(PAIR):
            whole(1 + c, send2.at[c], blocks - 1).wait_send()
        whole(1 + PAIR, send3, blocks - 1).wait_send()
        whole(2 + PAIR, send4, planes - 1).wait_send()

    @pl.when(jnp.logical_not(is_owner))
    def _():
        whole(0, send1, owners).wait_send()


def local(planes, blocks, outer_gate, inner_gate, signal, filter_taps, skip_gain):
    channels, tokens = signal.shape
    owners = planes // PAIR
    tables = make_tables(planes, blocks)
    bf16, f32 = jnp.bfloat16, jnp.float32
    scratch = [pltpu.VMEM((channels, tokens), bf16)] * 4
    scratch += [pltpu.SMEM((channels,), f32)]
    scratch += [pltpu.VMEM(t.shape, t.dtype) for t in tables]
    scratch += [
        pltpu.VMEM((channels, tokens), f32),
        pltpu.VMEM((channels * 2 * ROWS, LANES), f32),
        pltpu.VMEM((owners, PAIR * 2 * ROWS, LANES), bf16),
        pltpu.VMEM((planes, PAIR * 2 * ROWS, LANES), bf16),
        pltpu.VMEM((PAIR, blocks, 2 * ROWS, LANES), bf16),
        pltpu.VMEM((PAIR, blocks, 2 * ROWS, LANES), bf16),
    ]
    scratch += [pltpu.VMEM((blocks, ROWS, LANES), f32)] * 4
    scratch += [
        pltpu.VMEM((blocks, PAIR * ROWS, LANES), f32),
        pltpu.VMEM((blocks, PAIR * ROWS, LANES), bf16),
        pltpu.VMEM((blocks, PAIR * ROWS, LANES), bf16),
        pltpu.VMEM((planes, PAIR * ROWS, LANES), bf16),
        pltpu.VMEM((owners, PAIR * ROWS, LANES), bf16),
        pltpu.VMEM((channels * ROWS, LANES), f32),
        pltpu.SemaphoreType.DMA((11,)),
        pltpu.SemaphoreType.DMA((3 + PAIR,)),
        pltpu.SemaphoreType.DMA((3 + PAIR,)),
    ]
    operands = (inner_gate, signal, filter_taps, outer_gate, skip_gain, *[jnp.asarray(t) for t in tables])
    return pl.pallas_call(
        functools.partial(kernel, planes, blocks),
        out_shape=pltpu.VMEM((channels, tokens), bf16),
        in_specs=[pl.BlockSpec(memory_space=pltpu.HBM)] * len(operands),
        out_specs=pl.BlockSpec(memory_space=pltpu.VMEM),
        scratch_shapes=scratch,
        compiler_params=pltpu.CompilerParams(
            collective_id=0, has_side_effects=True, vmem_limit_bytes=16 * 2**20
        ),
        name="hyena_conv",
    )(*[pltpu.with_memory_space_constraint(operand, pltpu.HBM) for operand in operands])


def solution(mesh):
    spec = P(None, ("ctx", "ch"))
    return jax.shard_map(
        functools.partial(local, mesh.shape["ch"], mesh.shape["ctx"]),
        mesh=mesh,
        in_specs=(spec, spec, spec, spec, P()),
        out_specs=spec,
        check_vma=False,
    )
```

```python
import functools
import math

import jax
import jax.numpy as jnp
import ml_dtypes
import numpy as np
from jax import lax
from jax.experimental import pallas as pl
from jax.experimental.pallas import tpu as pltpu
from jax.sharding import PartitionSpec as P

MESH = pl.DeviceIdType.MESH
LANES = 128
ROWS = 8
PAIR = 2
DOUBLES_IN_EIGHT = 3


def split_bf16(table):
    high = table.astype(ml_dtypes.bfloat16)
    low = (table - high.astype(np.float64)).astype(ml_dtypes.bfloat16)
    return np.stack([high, low])


def make_tables(planes, blocks):
    units = ROWS * planes
    length = units * LANES
    part = units // blocks
    block, kind, row = np.meshgrid(np.arange(blocks), np.arange(2), np.arange(part), indexing="ij")
    row_first = (block * part + row).reshape(-1)
    row_kind = kind.reshape(-1)
    plane, column_kind, sub = np.meshgrid(np.arange(planes), np.arange(2), np.arange(ROWS), indexing="ij")
    unit = (plane * ROWS + sub).reshape(-1)
    column_kind = column_kind.reshape(-1)
    lane = np.arange(LANES)

    angle = 0.5 * np.pi * LANES * unit[None, :] / length
    angle = angle - 2 * np.pi * ((row_first[:, None] * unit[None, :]) % units) / units
    same = row_kind[:, None] == column_kind[None, :]
    first = np.concatenate([np.cos(angle) * same, np.sin(angle) * same])

    angle = 0.5 * np.pi * lane[None, :] / length - 2 * np.pi * row_first[:, None] * lane[None, :] / length
    twist = np.stack([np.cos(angle), np.sin(angle)])

    angle = 2 * np.pi * ((lane[:, None] * lane[None, :]) % LANES) / LANES
    cosine, sine = np.cos(angle), np.sin(angle)
    second = np.block([[cosine, -sine], [sine, cosine]])
    back = np.concatenate([cosine, sine], axis=1)

    real, imag = twist[0], -twist[1]
    is_real = row_kind[:, None] == 0
    untwist = np.stack([np.where(is_real, real, -imag), np.where(is_real, -imag, -real)])

    every_unit = np.arange(units)
    angle = -0.5 * np.pi * LANES * every_unit[:, None] / length
    angle = angle + 2 * np.pi * ((every_unit[:, None] * row_first[None, :]) % units) / units
    last = np.concatenate([np.cos(angle), -np.sin(angle)], axis=1) / length
    return (
        split_bf16(first),
        twist.astype(np.float32),
        split_bf16(second),
        back.astype(ml_dtypes.bfloat16),
        untwist.astype(np.float32),
        last.astype(ml_dtypes.bfloat16),
    )


def dot(left, right):
    return jnp.dot(left, right, preferred_element_type=jnp.float32)


def halves(value):
    high = value.astype(jnp.bfloat16)
    low = (value - high.astype(jnp.float32)).astype(jnp.bfloat16)
    return high, low


def away(k, size, ring):
    def around(k, n):
        return min(k, n - k)

    if ring:
        return around(k, size)
    side = max(1, math.isqrt(size // 2))
    return around(k // (2 * side), side) + around(k // 2 % side, side)


def far_first(size, ring):
    return sorted(range(1, size), key=lambda k: -away(k, size, ring))


def layout(planes):
    doubles = DOUBLES_IN_EIGHT * planes // 8
    return planes - PAIR * doubles, doubles


def kernel(planes, blocks, inner_hbm, signal_hbm, taps_hbm, outer_hbm, skip_hbm, first_hbm, twist_hbm,
           second_hbm, back_hbm, untwist_hbm, last_hbm, out_ref,
           inner, signal, taps, outer, skip_scalars, first, twist, second, back, untwist, last,
           mixed, staged, send1, recv1, send2, recv2, xa, xb, ha, hb, product, send3, recv3, send4, recv4, rows4,
           load_sem, send_sem, recv_sem):
    me = lax.axis_index("ctx")
    plane = lax.axis_index("ch")
    channels = planes
    singles, doubles = layout(planes)
    owners = singles + doubles

    def rank(z):
        return (z + singles) % planes

    units = ROWS * planes
    part = units // blocks
    is_owner = rank(plane) < owners
    mine = rank(plane)
    is_double = jnp.logical_and(mine >= singles, mine < owners)
    is_single = mine < singles
    ring = far_first(planes, True)
    flat = far_first(blocks, False)

    barrier = pltpu.get_barrier_semaphore()

    @pl.when(is_owner)
    def _():
        for k in ring:
            pl.semaphore_signal(barrier, inc=1, device_id=(me, (plane + k) % planes), device_id_type=MESH)
        for k in flat:
            pl.semaphore_signal(barrier, inc=1, device_id=((me + k) % blocks, plane), device_id_type=MESH)

    sources = (inner_hbm, signal_hbm, taps_hbm, outer_hbm, skip_hbm, first_hbm, twist_hbm, second_hbm,
               back_hbm, untwist_hbm, last_hbm)
    places = (inner, signal, taps, outer, skip_scalars, first, twist, second, back, untwist, last)
    loads = [pltpu.make_async_copy(s, d, load_sem.at[i]) for i, (s, d) in enumerate(zip(sources, places))]
    for load in loads[:5]:
        load.start()
    for load in loads[:3]:
        load.wait()

    gated = inner[...].astype(jnp.float32) * signal[...].astype(jnp.float32)
    gated = gated.astype(jnp.bfloat16).astype(jnp.float32)
    mixed[...] = gated
    filters = taps[...].astype(jnp.float32)
    for s in range(ROWS):
        columns = slice(s * LANES, (s + 1) * LANES)
        staged[pl.ds(s, channels, stride=2 * ROWS), :] = gated[:, columns]
        staged[pl.ds(ROWS + s, channels, stride=2 * ROWS), :] = filters[:, columns]
    send1[...] = staged[...].reshape(channels, 2 * ROWS, LANES).astype(jnp.bfloat16)

    pl.semaphore_wait(barrier, jnp.where(is_owner, owners + blocks - 2, owners))

    def remote(stage, source, target, device):
        return pltpu.make_async_remote_copy(
            src_ref=source,
            dst_ref=target,
            send_sem=send_sem.at[stage],
            recv_sem=recv_sem.at[stage],
            device_id=device,
            device_id_type=MESH,
        )

    def channel_of(owner):
        return singles + PAIR * (owner - singles)

    def whole(stage, buffer, slots):
        return remote(stage, buffer.at[pl.ds(0, slots)], buffer.at[pl.ds(0, slots)], (me, plane))

    for k in ring:
        there = (plane + k) % planes

        @pl.when(rank(there) < singles)
        def _(there=there):
            remote(0, send1.at[rank(there)], recv1.at[plane, 0], (me, there)).start()

        @pl.when(jnp.logical_and(rank(there) >= singles, rank(there) < owners))
        def _(there=there):
            remote(0, send1.at[pl.ds(channel_of(rank(there)), PAIR)], recv1.at[plane], (me, there)).start()

    @pl.when(is_owner)
    def _():
        for load in loads[5:]:
            load.start()

        @pl.when(is_single)
        def _():
            recv1[plane, 0] = send1[mine]

        @pl.when(is_double)
        def _():
            recv1[plane] = send1[pl.ds(channel_of(mine), PAIR)]

        for load in loads[5:]:
            load.wait()

        @pl.when(is_single)
        def _():
            whole(0, recv1.at[:, 0], planes - 1).wait_recv()

        @pl.when(is_double)
        def _():
            whole(0, recv1, planes - 1).wait_recv()

        values = jnp.concatenate([recv1[:, c].reshape(2 * units, LANES) for c in range(PAIR)], axis=1)
        along = dot(first[0], values) + dot(first[1], values)
        def forward(c):
            real = along[: 2 * units, c * LANES : (c + 1) * LANES]
            imag = along[2 * units :, c * LANES : (c + 1) * LANES]
            turned = jnp.concatenate(
                [real * twist[0] - imag * twist[1], real * twist[1] + imag * twist[0]], axis=1
            )
            high, low = halves(turned)
            spectrum = dot(high, second[0]) + dot(low, second[0]) + dot(high, second[1])
            send2[c] = jnp.concatenate(
                [
                    spectrum[:, :LANES].reshape(blocks, ROWS, LANES),
                    spectrum[:, LANES:].reshape(blocks, ROWS, LANES),
                ],
                axis=1,
            ).astype(jnp.bfloat16)
            recv2[c, me] = send2[c, me]
            for k in flat:
                there = (me + k) % blocks
                remote(1 + c, send2.at[c, there], recv2.at[c, me], (there, plane)).start()

        forward(0)
        pl.when(is_double)(functools.partial(forward, 1))

        upper = lax.broadcasted_iota(jnp.int32, (blocks, ROWS, LANES), 1) < part
        sign = jnp.where(lax.broadcasted_iota(jnp.int32, (ROWS, LANES), 0) < part, 1.0, -1.0)
        group = min(8, blocks)
        def multiply(c):
            whole(1 + c, recv2.at[c], blocks - 1).wait_recv()
            pieces = recv2[c].astype(jnp.float32)
            real, imag = pieces[:, :ROWS], pieces[:, ROWS:]
            real_rolled = jnp.roll(real, part, axis=1)
            imag_rolled = jnp.roll(imag, part, axis=1)
            xa[...] = jnp.where(upper, real, imag_rolled)
            xb[...] = jnp.where(upper, imag, real_rolled)
            ha[...] = jnp.where(upper, real_rolled, real)
            hb[...] = jnp.where(upper, -imag_rolled, imag)
            before = jnp.zeros((ROWS, LANES), jnp.float32)
            for start in range(0, blocks, group):
                sums = [jnp.zeros((ROWS, LANES), jnp.float32) for _ in range(group)]
                for i in range(start + group):
                    x_direct, x_crossed = xa[i], xb[i]
                    for offset in range(group):
                        j = start + offset - i
                        if j >= 0:
                            sums[offset] = sums[offset] + (x_direct * ha[j] + x_crossed * hb[j])
                for offset in range(group):
                    product[start + offset, c * ROWS : (c + 1) * ROWS, :] = sums[offset] + sign * jnp.roll(
                        before, part, axis=0
                    )
                    before = sums[offset]

        multiply(0)
        pl.when(is_double)(functools.partial(multiply, 1))

        @pl.when(is_single)
        def _():
            product[:, ROWS:, :] = jnp.zeros((blocks, ROWS, LANES), jnp.float32)

        send3[...] = product[...].astype(jnp.bfloat16)
        recv3[me] = send3[me]
        for there in sorted(range(blocks), key=lambda k: away(k, blocks, False)):

            @pl.when(there != me)
            def _(there=there):
                remote(1 + PAIR, send3.at[there], recv3.at[me], (there, plane)).start()
        whole(1 + PAIR, recv3, blocks - 1).wait_recv()

        waves = recv3[...].reshape(blocks * PAIR * ROWS, LANES)
        lanes_back = dot(waves, back[...]).reshape(blocks, PAIR, ROWS, 2 * LANES)
        turned = []
        for c in range(PAIR):
            lanes_c = lanes_back[:, c].reshape(2 * units, 2 * LANES)
            first_half, second_half = lanes_c[:, :LANES], lanes_c[:, LANES:]
            turned.append(
                jnp.concatenate(
                    [
                        first_half * untwist[0] + second_half * untwist[1],
                        second_half * untwist[0] - first_half * untwist[1],
                    ],
                    axis=0,
                )
            )
        result = dot(last[...], jnp.concatenate(turned, axis=1).astype(jnp.bfloat16))
        send4[...] = jnp.concatenate(
            [result[:, c * LANES : (c + 1) * LANES].reshape(planes, ROWS, LANES) for c in range(PAIR)], axis=1
        ).astype(jnp.bfloat16)
        recv4[mine] = send4[plane]
        for k in ring:
            there = (plane + k) % planes
            if 1: continue
            remote(2 + PAIR, send4.at[there], recv4.at[mine], (me, there)).start()

        for there in range(planes):

            @pl.when(there != plane)
            def _(there=there):
                remote(2 + PAIR, send4.at[there], recv4.at[mine], (me, there)).start()

    channel = lax.broadcasted_iota(jnp.int32, (channels, LANES), 0)
    loads[3].wait()
    loads[4].wait()
    skip = jnp.zeros((channels, LANES), jnp.float32)
    for c in range(channels):
        skip = jnp.where(channel == c, skip_scalars[c], skip)

    @pl.when(is_owner)
    def _():
        whole(2 + PAIR, recv4, owners - 1).wait_recv()

    @pl.when(jnp.logical_not(is_owner))
    def _():
        whole(2 + PAIR, recv4, owners).wait_recv()

    arrived = recv4[...].astype(jnp.float32)
    rows4[: singles * ROWS, :] = arrived[:singles, :ROWS, :].reshape(singles * ROWS, LANES)
    rows4[singles * ROWS :, :] = arrived[singles:].reshape((channels - singles) * ROWS, LANES)
    for s in range(ROWS):
        columns = slice(s * LANES, (s + 1) * LANES)
        conv = rows4[pl.ds(s, channels, stride=ROWS), :]
        total = conv + skip * mixed[:, columns]
        out_ref[:, columns] = (outer[:, columns].astype(jnp.float32) * total).astype(jnp.bfloat16)

    @pl.when(is_owner)
    def _():
        whole(1, send2.at[0], blocks - 1).wait_send()
        whole(1 + PAIR, send3, blocks - 1).wait_send()
        whole(2 + PAIR, send4, planes - 1).wait_send()

    @pl.when(is_single)
    def _():
        whole(0, send1, channels - 1).wait_send()

    @pl.when(is_double)
    def _():
        whole(0, send1, channels - PAIR).wait_send()
        whole(2, send2.at[1], blocks - 1).wait_send()

    @pl.when(jnp.logical_not(is_owner))
    def _():
        whole(0, send1, channels).wait_send()


def local(planes, blocks, outer_gate, inner_gate, signal, filter_taps, skip_gain):
    channels, tokens = signal.shape
    owners = sum(layout(planes))
    tables = make_tables(planes, blocks)
    bf16, f32 = jnp.bfloat16, jnp.float32
    scratch = [pltpu.VMEM((channels, tokens), bf16)] * 4
    scratch += [pltpu.SMEM((channels,), f32)]
    scratch += [pltpu.VMEM(t.shape, t.dtype) for t in tables]
    scratch += [
        pltpu.VMEM((channels, tokens), f32),
        pltpu.VMEM((channels * 2 * ROWS, LANES), f32),
        pltpu.VMEM((channels, 2 * ROWS, LANES), bf16),
        pltpu.VMEM((planes, PAIR, 2 * ROWS, LANES), bf16),
        pltpu.VMEM((PAIR, blocks, 2 * ROWS, LANES), bf16),
        pltpu.VMEM((PAIR, blocks, 2 * ROWS, LANES), bf16),
    ]
    scratch += [pltpu.VMEM((blocks, ROWS, LANES), f32)] * 4
    scratch += [
        pltpu.VMEM((blocks, PAIR * ROWS, LANES), f32),
        pltpu.VMEM((blocks, PAIR * ROWS, LANES), bf16),
        pltpu.VMEM((blocks, PAIR * ROWS, LANES), bf16),
        pltpu.VMEM((planes, PAIR * ROWS, LANES), bf16),
        pltpu.VMEM((owners, PAIR * ROWS, LANES), bf16),
        pltpu.VMEM((channels * ROWS, LANES), f32),
        pltpu.SemaphoreType.DMA((11,)),
        pltpu.SemaphoreType.DMA((3 + PAIR,)),
        pltpu.SemaphoreType.DMA((3 + PAIR,)),
    ]
    operands = (inner_gate, signal, filter_taps, outer_gate, skip_gain, *[jnp.asarray(t) for t in tables])
    return pl.pallas_call(
        functools.partial(kernel, planes, blocks),
        out_shape=pltpu.VMEM((channels, tokens), bf16),
        in_specs=[pl.BlockSpec(memory_space=pltpu.HBM)] * len(operands),
        out_specs=pl.BlockSpec(memory_space=pltpu.VMEM),
        scratch_shapes=scratch,
        compiler_params=pltpu.CompilerParams(
            collective_id=0, has_side_effects=True, vmem_limit_bytes=16 * 2**20
        ),
        name="hyena_conv",
    )(*[pltpu.with_memory_space_constraint(operand, pltpu.HBM) for operand in operands])


def solution(mesh):
    spec = P(None, ("ctx", "ch"))
    return jax.shard_map(
        functools.partial(local, mesh.shape["ch"], mesh.shape["ctx"]),
        mesh=mesh,
        in_specs=(spec, spec, spec, spec, P()),
        out_specs=spec,
        check_vma=False,
    )
```

```python
import functools
import math

import jax
import jax.numpy as jnp
import ml_dtypes
import numpy as np
from jax import lax
from jax.experimental import pallas as pl
from jax.experimental.pallas import tpu as pltpu
from jax.sharding import PartitionSpec as P

MESH = pl.DeviceIdType.MESH
LANES = 128
ROWS = 8
PAIR = 2


def split_bf16(table):
    high = table.astype(ml_dtypes.bfloat16)
    low = (table - high.astype(np.float64)).astype(ml_dtypes.bfloat16)
    return np.stack([high, low])


def make_tables(planes, blocks):
    units = ROWS * planes
    length = units * LANES
    part = units // blocks
    block, kind, row = np.meshgrid(np.arange(blocks), np.arange(2), np.arange(part), indexing="ij")
    row_first = (block * part + row).reshape(-1)
    row_kind = kind.reshape(-1)
    plane, column_kind, sub = np.meshgrid(np.arange(planes), np.arange(2), np.arange(ROWS), indexing="ij")
    unit = (plane * ROWS + sub).reshape(-1)
    column_kind = column_kind.reshape(-1)
    lane = np.arange(LANES)

    angle = 0.5 * np.pi * LANES * unit[None, :] / length
    angle = angle - 2 * np.pi * ((row_first[:, None] * unit[None, :]) % units) / units
    same = row_kind[:, None] == column_kind[None, :]
    first = np.concatenate([np.cos(angle) * same, np.sin(angle) * same])

    angle = 0.5 * np.pi * lane[None, :] / length - 2 * np.pi * row_first[:, None] * lane[None, :] / length
    twist = np.stack([np.cos(angle), np.sin(angle)])

    angle = 2 * np.pi * ((lane[:, None] * lane[None, :]) % LANES) / LANES
    cosine, sine = np.cos(angle), np.sin(angle)
    second = np.block([[cosine, -sine], [sine, cosine]])
    back = np.concatenate([cosine, sine], axis=1)

    real, imag = twist[0], -twist[1]
    is_real = row_kind[:, None] == 0
    untwist = np.stack([np.where(is_real, real, -imag), np.where(is_real, -imag, -real)])

    every_unit = np.arange(units)
    angle = -0.5 * np.pi * LANES * every_unit[:, None] / length
    angle = angle + 2 * np.pi * ((every_unit[:, None] * row_first[None, :]) % units) / units
    last = np.concatenate([np.cos(angle), -np.sin(angle)], axis=1) / length
    return (
        split_bf16(first),
        twist.astype(np.float32),
        split_bf16(second),
        back.astype(ml_dtypes.bfloat16),
        untwist.astype(np.float32),
        last.astype(ml_dtypes.bfloat16),
    )


def dot(left, right):
    return jnp.dot(left, right, preferred_element_type=jnp.float32)


def halves(value):
    high = value.astype(jnp.bfloat16)
    low = (value - high.astype(jnp.float32)).astype(jnp.bfloat16)
    return high, low


def away(k, size, ring):
    def around(k, n):
        return min(k, n - k)

    if ring:
        return around(k, size)
    side = max(1, math.isqrt(size // 2))
    return around(k // (2 * side), side) + around(k // 2 % side, side)


def far_first(size, ring):
    return sorted(range(1, size), key=lambda k: -away(k, size, ring))


def layout(planes):
    quarter = planes // 4
    return quarter, quarter, quarter


def kernel(planes, blocks, inner_hbm, signal_hbm, taps_hbm, outer_hbm, skip_hbm, first_hbm, twist_hbm,
           second_hbm, back_hbm, untwist_hbm, last_hbm, out_ref,
           inner, signal, taps, outer, skip_scalars, first, twist, second, back, untwist, last,
           mixed, staged, send1, recv1, send2, recv2, xa, xb, ha, hb, product, send3, recv3, send4, recv4, rows4,
           load_sem, send_sem, recv_sem):
    me = lax.axis_index("ctx")
    plane = lax.axis_index("ch")
    channels = planes
    ahead, doubles, behind = layout(planes)
    owners = ahead + doubles + behind


    def rank(z):
        return (z + ahead) % planes

    def has_two(owner):
        return jnp.logical_and(owner >= ahead, owner < ahead + doubles)

    def has_one(owner):
        return jnp.logical_and(owner < owners, jnp.logical_not(has_two(owner)))

    def channel_of(owner):
        return owner + jnp.clip(owner - ahead, 0, doubles)

    units = ROWS * planes
    part = units // blocks
    is_owner = rank(plane) < owners
    mine = rank(plane)
    is_double = has_two(mine)
    is_single = has_one(mine)
    ring = far_first(planes, True)
    flat = far_first(blocks, False)

    barrier = pltpu.get_barrier_semaphore()

    @pl.when(is_owner)
    def _():
        for k in ring:
            pl.semaphore_signal(barrier, inc=1, device_id=(me, (plane + k) % planes), device_id_type=MESH)
        for k in flat:
            pl.semaphore_signal(barrier, inc=1, device_id=((me + k) % blocks, plane), device_id_type=MESH)

    sources = (inner_hbm, signal_hbm, taps_hbm, outer_hbm, skip_hbm, first_hbm, twist_hbm, second_hbm,
               back_hbm, untwist_hbm, last_hbm)
    places = (inner, signal, taps, outer, skip_scalars, first, twist, second, back, untwist, last)
    loads = [pltpu.make_async_copy(s, d, load_sem.at[i]) for i, (s, d) in enumerate(zip(sources, places))]
    for load in loads[:5]:
        load.start()
    for load in loads[:3]:
        load.wait()

    gated = inner[...].astype(jnp.float32) * signal[...].astype(jnp.float32)
    gated = gated.astype(jnp.bfloat16).astype(jnp.float32)
    mixed[...] = gated
    filters = taps[...].astype(jnp.float32)
    for s in range(ROWS):
        columns = slice(s * LANES, (s + 1) * LANES)
        staged[pl.ds(s, channels, stride=2 * ROWS), :] = gated[:, columns]
        staged[pl.ds(ROWS + s, channels, stride=2 * ROWS), :] = filters[:, columns]
    send1[...] = staged[...].reshape(channels, 2 * ROWS, LANES).astype(jnp.bfloat16)

    pl.semaphore_wait(barrier, jnp.where(is_owner, owners + blocks - 2, owners))

    def remote(stage, source, target, device):
        return pltpu.make_async_remote_copy(
            src_ref=source,
            dst_ref=target,
            send_sem=send_sem.at[stage],
            recv_sem=recv_sem.at[stage],
            device_id=device,
            device_id_type=MESH,
        )

    def whole(stage, buffer, slots):
        return remote(stage, buffer.at[pl.ds(0, slots)], buffer.at[pl.ds(0, slots)], (me, plane))

    for k in ring:
        there = (plane + k) % planes

        @pl.when(has_one(rank(there)))
        def _(there=there):
            remote(0, send1.at[channel_of(rank(there))], recv1.at[plane, 0], (me, there)).start()

        @pl.when(has_two(rank(there)))
        def _(there=there):
            remote(0, send1.at[pl.ds(channel_of(rank(there)), PAIR)], recv1.at[plane], (me, there)).start()

    @pl.when(is_owner)
    def _():
        for load in loads[5:]:
            load.start()

        @pl.when(is_single)
        def _():
            recv1[plane, 0] = send1[channel_of(mine)]

        @pl.when(is_double)
        def _():
            recv1[plane] = send1[pl.ds(channel_of(mine), PAIR)]

        for load in loads[5:]:
            load.wait()

        @pl.when(is_single)
        def _():
            whole(0, recv1.at[:, 0], planes - 1).wait_recv()

        @pl.when(is_double)
        def _():
            whole(0, recv1, planes - 1).wait_recv()

        values = jnp.concatenate([recv1[:, c].reshape(2 * units, LANES) for c in range(PAIR)], axis=1)
        along = dot(first[0], values) + dot(first[1], values)
        def forward(c):
            real = along[: 2 * units, c * LANES : (c + 1) * LANES]
            imag = along[2 * units :, c * LANES : (c + 1) * LANES]
            turned = jnp.concatenate(
                [real * twist[0] - imag * twist[1], real * twist[1] + imag * twist[0]], axis=1
            )
            high, low = halves(turned)
            spectrum = dot(high, second[0]) + dot(low, second[0]) + dot(high, second[1])
            send2[c] = jnp.concatenate(
                [
                    spectrum[:, :LANES].reshape(blocks, ROWS, LANES),
                    spectrum[:, LANES:].reshape(blocks, ROWS, LANES),
                ],
                axis=1,
            ).astype(jnp.bfloat16)
            recv2[c, me] = send2[c, me]
            for k in flat:
                there = (me + k) % blocks
                remote(1 + c, send2.at[c, there], recv2.at[c, me], (there, plane)).start()

        forward(0)
        pl.when(is_double)(functools.partial(forward, 1))

        upper = lax.broadcasted_iota(jnp.int32, (blocks, ROWS, LANES), 1) < part
        sign = jnp.where(lax.broadcasted_iota(jnp.int32, (ROWS, LANES), 0) < part, 1.0, -1.0)
        group = min(8, blocks)
        def multiply(c):
            whole(1 + c, recv2.at[c], blocks - 1).wait_recv()
            pieces = recv2[c].astype(jnp.float32)
            real, imag = pieces[:, :ROWS], pieces[:, ROWS:]
            real_rolled = jnp.roll(real, part, axis=1)
            imag_rolled = jnp.roll(imag, part, axis=1)
            xa[...] = jnp.where(upper, real, imag_rolled)
            xb[...] = jnp.where(upper, imag, real_rolled)
            ha[...] = jnp.where(upper, real_rolled, real)
            hb[...] = jnp.where(upper, -imag_rolled, imag)
            before = jnp.zeros((ROWS, LANES), jnp.float32)
            for start in range(0, blocks, group):
                sums = [jnp.zeros((ROWS, LANES), jnp.float32) for _ in range(group)]
                for i in range(start + group):
                    x_direct, x_crossed = xa[i], xb[i]
                    for offset in range(group):
                        j = start + offset - i
                        if j >= 0:
                            sums[offset] = sums[offset] + (x_direct * ha[j] + x_crossed * hb[j])
                for offset in range(group):
                    product[start + offset, c * ROWS : (c + 1) * ROWS, :] = sums[offset] + sign * jnp.roll(
                        before, part, axis=0
                    )
                    before = sums[offset]

        multiply(0)
        pl.when(is_double)(functools.partial(multiply, 1))

        @pl.when(is_single)
        def _():
            product[:, ROWS:, :] = jnp.zeros((blocks, ROWS, LANES), jnp.float32)

        send3[...] = product[...].astype(jnp.bfloat16)
        recv3[me] = send3[me]
        for there in sorted(range(blocks), key=lambda k: away(k, blocks, False)):

            @pl.when(there != me)
            def _(there=there):
                remote(1 + PAIR, send3.at[there], recv3.at[me], (there, plane)).start()
        whole(1 + PAIR, recv3, blocks - 1).wait_recv()

        waves = recv3[...].reshape(blocks * PAIR * ROWS, LANES)
        lanes_back = dot(waves, back[...]).reshape(blocks, PAIR, ROWS, 2 * LANES)
        turned = []
        for c in range(PAIR):
            lanes_c = lanes_back[:, c].reshape(2 * units, 2 * LANES)
            first_half, second_half = lanes_c[:, :LANES], lanes_c[:, LANES:]
            turned.append(
                jnp.concatenate(
                    [
                        first_half * untwist[0] + second_half * untwist[1],
                        second_half * untwist[0] - first_half * untwist[1],
                    ],
                    axis=0,
                )
            )
        result = dot(last[...], jnp.concatenate(turned, axis=1).astype(jnp.bfloat16))
        send4[...] = jnp.concatenate(
            [result[:, c * LANES : (c + 1) * LANES].reshape(planes, ROWS, LANES) for c in range(PAIR)], axis=1
        ).astype(jnp.bfloat16)
        recv4[mine] = send4[plane]
        for k in ring:
            there = (plane + k) % planes
            if 1: continue
            remote(2 + PAIR, send4.at[there], recv4.at[mine], (me, there)).start()

        for there in range(planes):

            @pl.when(there != plane)
            def _(there=there):
                remote(2 + PAIR, send4.at[there], recv4.at[mine], (me, there)).start()

    channel = lax.broadcasted_iota(jnp.int32, (channels, LANES), 0)
    loads[3].wait()
    loads[4].wait()
    skip = jnp.zeros((channels, LANES), jnp.float32)
    for c in range(channels):
        skip = jnp.where(channel == c, skip_scalars[c], skip)

    @pl.when(is_owner)
    def _():
        whole(2 + PAIR, recv4, owners - 1).wait_recv()

    @pl.when(jnp.logical_not(is_owner))
    def _():
        whole(2 + PAIR, recv4, owners).wait_recv()

    arrived = recv4[...].astype(jnp.float32)
    row = 0
    for owner in range(owners):
        rows = PAIR * ROWS if ahead <= owner < ahead + doubles else ROWS
        rows4[row : row + rows, :] = arrived[owner, :rows, :]
        row += rows
    for s in range(ROWS):
        columns = slice(s * LANES, (s + 1) * LANES)
        conv = rows4[pl.ds(s, channels, stride=ROWS), :]
        total = conv + skip * mixed[:, columns]
        out_ref[:, columns] = (outer[:, columns].astype(jnp.float32) * total).astype(jnp.bfloat16)

    @pl.when(is_owner)
    def _():
        whole(1, send2.at[0], blocks - 1).wait_send()
        whole(1 + PAIR, send3, blocks - 1).wait_send()
        whole(2 + PAIR, send4, planes - 1).wait_send()

    @pl.when(is_single)
    def _():
        whole(0, send1, channels - 1).wait_send()

    @pl.when(is_double)
    def _():
        whole(0, send1, channels - PAIR).wait_send()
        whole(2, send2.at[1], blocks - 1).wait_send()

    @pl.when(jnp.logical_not(is_owner))
    def _():
        whole(0, send1, channels).wait_send()


def local(planes, blocks, outer_gate, inner_gate, signal, filter_taps, skip_gain):
    channels, tokens = signal.shape
    owners = sum(layout(planes))
    tables = make_tables(planes, blocks)
    bf16, f32 = jnp.bfloat16, jnp.float32
    scratch = [pltpu.VMEM((channels, tokens), bf16)] * 4
    scratch += [pltpu.SMEM((channels,), f32)]
    scratch += [pltpu.VMEM(t.shape, t.dtype) for t in tables]
    scratch += [
        pltpu.VMEM((channels, tokens), f32),
        pltpu.VMEM((channels * 2 * ROWS, LANES), f32),
        pltpu.VMEM((channels, 2 * ROWS, LANES), bf16),
        pltpu.VMEM((planes, PAIR, 2 * ROWS, LANES), bf16),
        pltpu.VMEM((PAIR, blocks, 2 * ROWS, LANES), bf16),
        pltpu.VMEM((PAIR, blocks, 2 * ROWS, LANES), bf16),
    ]
    scratch += [pltpu.VMEM((blocks, ROWS, LANES), f32)] * 4
    scratch += [
        pltpu.VMEM((blocks, PAIR * ROWS, LANES), f32),
        pltpu.VMEM((blocks, PAIR * ROWS, LANES), bf16),
        pltpu.VMEM((blocks, PAIR * ROWS, LANES), bf16),
        pltpu.VMEM((planes, PAIR * ROWS, LANES), bf16),
        pltpu.VMEM((owners, PAIR * ROWS, LANES), bf16),
        pltpu.VMEM((channels * ROWS, LANES), f32),
        pltpu.SemaphoreType.DMA((11,)),
        pltpu.SemaphoreType.DMA((3 + PAIR,)),
        pltpu.SemaphoreType.DMA((3 + PAIR,)),
    ]
    operands = (inner_gate, signal, filter_taps, outer_gate, skip_gain, *[jnp.asarray(t) for t in tables])
    return pl.pallas_call(
        functools.partial(kernel, planes, blocks),
        out_shape=pltpu.VMEM((channels, tokens), bf16),
        in_specs=[pl.BlockSpec(memory_space=pltpu.HBM)] * len(operands),
        out_specs=pl.BlockSpec(memory_space=pltpu.VMEM),
        scratch_shapes=scratch,
        compiler_params=pltpu.CompilerParams(
            collective_id=0, has_side_effects=True, vmem_limit_bytes=16 * 2**20
        ),
        name="hyena_conv",
    )(*[pltpu.with_memory_space_constraint(operand, pltpu.HBM) for operand in operands])


def solution(mesh):
    spec = P(None, ("ctx", "ch"))
    return jax.shard_map(
        functools.partial(local, mesh.shape["ch"], mesh.shape["ctx"]),
        mesh=mesh,
        in_specs=(spec, spec, spec, spec, P()),
        out_specs=spec,
        check_vma=False,
    )
```

```python
import functools
import math

import jax
import jax.numpy as jnp
import ml_dtypes
import numpy as np
from jax import lax
from jax.experimental import pallas as pl
from jax.experimental.pallas import tpu as pltpu
from jax.sharding import PartitionSpec as P

MESH = pl.DeviceIdType.MESH
LANES = 128
ROWS = 8
PAIR = 2


def split_bf16(table):
    high = table.astype(ml_dtypes.bfloat16)
    low = (table - high.astype(np.float64)).astype(ml_dtypes.bfloat16)
    return np.stack([high, low])


def make_tables(planes, blocks):
    units = ROWS * planes
    length = units * LANES
    part = units // blocks
    block, kind, row = np.meshgrid(np.arange(blocks), np.arange(2), np.arange(part), indexing="ij")
    row_first = (block * part + row).reshape(-1)
    row_kind = kind.reshape(-1)
    plane, column_kind, sub = np.meshgrid(np.arange(planes), np.arange(2), np.arange(ROWS), indexing="ij")
    unit = (plane * ROWS + sub).reshape(-1)
    column_kind = column_kind.reshape(-1)
    lane = np.arange(LANES)

    angle = 0.5 * np.pi * LANES * unit[None, :] / length
    angle = angle - 2 * np.pi * ((row_first[:, None] * unit[None, :]) % units) / units
    same = row_kind[:, None] == column_kind[None, :]
    first = np.concatenate([np.cos(angle) * same, np.sin(angle) * same])

    angle = 0.5 * np.pi * lane[None, :] / length - 2 * np.pi * row_first[:, None] * lane[None, :] / length
    twist = np.stack([np.cos(angle), np.sin(angle)])

    angle = 2 * np.pi * ((lane[:, None] * lane[None, :]) % LANES) / LANES
    cosine, sine = np.cos(angle), np.sin(angle)
    second = np.block([[cosine, -sine], [sine, cosine]])
    back = np.concatenate([cosine, sine], axis=1)

    real, imag = twist[0], -twist[1]
    is_real = row_kind[:, None] == 0
    untwist = np.stack([np.where(is_real, real, -imag), np.where(is_real, -imag, -real)])

    every_unit = np.arange(units)
    angle = -0.5 * np.pi * LANES * every_unit[:, None] / length
    angle = angle + 2 * np.pi * ((every_unit[:, None] * row_first[None, :]) % units) / units
    last = np.concatenate([np.cos(angle), -np.sin(angle)], axis=1) / length
    return (
        split_bf16(first),
        twist.astype(np.float32),
        split_bf16(second),
        back.astype(ml_dtypes.bfloat16),
        untwist.astype(np.float32),
        last.astype(ml_dtypes.bfloat16),
    )


def dot(left, right):
    return jnp.dot(left, right, preferred_element_type=jnp.float32)


def halves(value):
    high = value.astype(jnp.bfloat16)
    low = (value - high.astype(jnp.float32)).astype(jnp.bfloat16)
    return high, low


def away(k, size, ring):
    def around(k, n):
        return min(k, n - k)

    if ring:
        return around(k, size)
    side = max(1, math.isqrt(size // 2))
    return around(k // (2 * side), side) + around(k // 2 % side, side)


def far_first(size, ring):
    return sorted(range(1, size), key=lambda k: -away(k, size, ring))


def layout(planes):
    quarter = planes // 4
    return quarter, quarter, quarter


def wrap(position, size):
    return lax.rem(position, jnp.int32(size))


def kernel(planes, blocks, inner_hbm, signal_hbm, taps_hbm, outer_hbm, skip_hbm, first_hbm, twist_hbm,
           second_hbm, back_hbm, untwist_hbm, last_hbm, out_ref,
           inner, signal, taps, outer, skip_scalars, first, twist, second, back, untwist, last,
           mixed, staged, send1, recv1, send2, recv2, xa, xb, ha, hb, product, send3, recv3, send4, recv4, rows4,
           load_sem, send_sem, recv_sem):
    me = lax.axis_index("ctx")
    plane = lax.axis_index("ch")
    channels = planes
    ahead, doubles, behind = layout(planes)
    owners = ahead + doubles + behind


    def rank(z):
        return wrap(z + ahead, planes)

    def has_two(owner):
        return jnp.logical_and(owner >= ahead, owner < ahead + doubles)

    def has_one(owner):
        return jnp.logical_and(owner < owners, jnp.logical_not(has_two(owner)))

    def channel_of(owner):
        return owner + jnp.clip(owner - ahead, 0, doubles)

    units = ROWS * planes
    part = units // blocks
    is_owner = rank(plane) < owners
    mine = rank(plane)
    is_double = has_two(mine)
    is_single = has_one(mine)
    ring = far_first(planes, True)
    flat = far_first(blocks, False)

    barrier = pltpu.get_barrier_semaphore()

    sources = (inner_hbm, signal_hbm, taps_hbm, outer_hbm, skip_hbm, first_hbm, twist_hbm, second_hbm,
               back_hbm, untwist_hbm, last_hbm)
    places = (inner, signal, taps, outer, skip_scalars, first, twist, second, back, untwist, last)
    loads = [pltpu.make_async_copy(s, d, load_sem.at[i]) for i, (s, d) in enumerate(zip(sources, places))]
    for load in loads[:3]:
        load.start()

    @pl.when(is_owner)
    def _():
        for k in ring:
            pl.semaphore_signal(barrier, inc=1, device_id=(me, wrap(plane + k, planes)), device_id_type=MESH)
        for k in flat:
            pl.semaphore_signal(barrier, inc=1, device_id=(wrap(me + k, blocks), plane), device_id_type=MESH)

    for load in loads[3:5]:
        load.start()
    for load in loads[:3]:
        load.wait()

    gated = inner[...].astype(jnp.float32) * signal[...].astype(jnp.float32)
    gated = gated.astype(jnp.bfloat16).astype(jnp.float32)
    mixed[...] = gated
    filters = taps[...].astype(jnp.float32)
    for s in range(ROWS):
        columns = slice(s * LANES, (s + 1) * LANES)
        staged[pl.ds(s, channels, stride=2 * ROWS), :] = gated[:, columns]
        staged[pl.ds(ROWS + s, channels, stride=2 * ROWS), :] = filters[:, columns]
    send1[...] = staged[...].reshape(channels, 2 * ROWS, LANES).astype(jnp.bfloat16)

    pl.semaphore_wait(barrier, jnp.where(is_owner, owners + blocks - 2, owners))

    def remote(stage, source, target, device):
        return pltpu.make_async_remote_copy(
            src_ref=source,
            dst_ref=target,
            send_sem=send_sem.at[stage],
            recv_sem=recv_sem.at[stage],
            device_id=device,
            device_id_type=MESH,
        )

    def whole(stage, buffer, slots):
        return remote(stage, buffer.at[pl.ds(0, slots)], buffer.at[pl.ds(0, slots)], (me, plane))

    for k in ring:
        there = wrap(plane + k, planes)

        @pl.when(has_one(rank(there)))
        def _(there=there):
            remote(0, send1.at[channel_of(rank(there))], recv1.at[plane, 0], (me, there)).start()

        @pl.when(has_two(rank(there)))
        def _(there=there):
            remote(0, send1.at[pl.ds(channel_of(rank(there)), PAIR)], recv1.at[plane], (me, there)).start()

    @pl.when(is_owner)
    def _():
        for load in loads[5:]:
            load.start()

        @pl.when(is_single)
        def _():
            recv1[plane, 0] = send1[channel_of(mine)]

        @pl.when(is_double)
        def _():
            recv1[plane] = send1[pl.ds(channel_of(mine), PAIR)]

        for load in loads[5:]:
            load.wait()

        @pl.when(is_single)
        def _():
            whole(0, recv1.at[:, 0], planes - 1).wait_recv()

        @pl.when(is_double)
        def _():
            whole(0, recv1, planes - 1).wait_recv()

        values = jnp.concatenate([recv1[:, c].reshape(2 * units, LANES) for c in range(PAIR)], axis=1)
        along = dot(first[0], values) + dot(first[1], values)
        def forward(c):
            real = along[: 2 * units, c * LANES : (c + 1) * LANES]
            imag = along[2 * units :, c * LANES : (c + 1) * LANES]
            turned = jnp.concatenate(
                [real * twist[0] - imag * twist[1], real * twist[1] + imag * twist[0]], axis=1
            )
            high, low = halves(turned)
            spectrum = dot(high, second[0]) + dot(low, second[0]) + dot(high, second[1])
            send2[c] = jnp.concatenate(
                [
                    spectrum[:, :LANES].reshape(blocks, ROWS, LANES),
                    spectrum[:, LANES:].reshape(blocks, ROWS, LANES),
                ],
                axis=1,
            ).astype(jnp.bfloat16)
            recv2[c, me] = send2[c, me]
            for k in flat:
                there = wrap(me + k, blocks)
                remote(1 + c, send2.at[c, there], recv2.at[c, me], (there, plane)).start()

        forward(0)
        pl.when(is_double)(functools.partial(forward, 1))

        upper = lax.broadcasted_iota(jnp.int32, (blocks, ROWS, LANES), 1) < part
        sign = jnp.where(lax.broadcasted_iota(jnp.int32, (ROWS, LANES), 0) < part, 1.0, -1.0)
        group = min(8, blocks)
        def multiply(c):
            whole(1 + c, recv2.at[c], blocks - 1).wait_recv()
            pieces = recv2[c].astype(jnp.float32)
            real, imag = pieces[:, :ROWS], pieces[:, ROWS:]
            real_rolled = jnp.roll(real, part, axis=1)
            imag_rolled = jnp.roll(imag, part, axis=1)
            xa[...] = jnp.where(upper, real, imag_rolled)
            xb[...] = jnp.where(upper, imag, real_rolled)
            ha[...] = jnp.where(upper, real_rolled, real)
            hb[...] = jnp.where(upper, -imag_rolled, imag)
            before = jnp.zeros((ROWS, LANES), jnp.float32)
            for start in range(0, blocks, group):
                sums = [jnp.zeros((ROWS, LANES), jnp.float32) for _ in range(group)]
                for i in range(start + group):
                    x_direct, x_crossed = xa[i], xb[i]
                    for offset in range(group):
                        j = start + offset - i
                        if j >= 0:
                            sums[offset] = sums[offset] + (x_direct * ha[j] + x_crossed * hb[j])
                for offset in range(group):
                    product[start + offset, c * ROWS : (c + 1) * ROWS, :] = sums[offset] + sign * jnp.roll(
                        before, part, axis=0
                    )
                    before = sums[offset]

        multiply(0)
        pl.when(is_double)(functools.partial(multiply, 1))

        @pl.when(is_single)
        def _():
            product[:, ROWS:, :] = jnp.zeros((blocks, ROWS, LANES), jnp.float32)

        send3[...] = product[...].astype(jnp.bfloat16)
        recv3[me] = send3[me]
        for there in sorted(range(blocks), key=lambda k: away(k, blocks, False)):

            @pl.when(there != me)
            def _(there=there):
                remote(1 + PAIR, send3.at[there], recv3.at[me], (there, plane)).start()
        whole(1 + PAIR, recv3, blocks - 1).wait_recv()

        waves = recv3[...].reshape(blocks * PAIR * ROWS, LANES)
        lanes_back = dot(waves, back[...]).reshape(blocks, PAIR, ROWS, 2 * LANES)
        turned = []
        for c in range(PAIR):
            lanes_c = lanes_back[:, c].reshape(2 * units, 2 * LANES)
            first_half, second_half = lanes_c[:, :LANES], lanes_c[:, LANES:]
            turned.append(
                jnp.concatenate(
                    [
                        first_half * untwist[0] + second_half * untwist[1],
                        second_half * untwist[0] - first_half * untwist[1],
                    ],
                    axis=0,
                )
            )
        result = dot(last[...], jnp.concatenate(turned, axis=1).astype(jnp.bfloat16))
        send4[...] = jnp.concatenate(
            [result[:, c * LANES : (c + 1) * LANES].reshape(planes, ROWS, LANES) for c in range(PAIR)], axis=1
        ).astype(jnp.bfloat16)
        recv4[mine] = send4[plane]
        for k in ring:
            there = wrap(plane + k, planes)
            if 1: continue
            remote(2 + PAIR, send4.at[there], recv4.at[mine], (me, there)).start()

        def deliver(targets, stage):
            for there in targets:

                @pl.when(there != plane)
                def _(there=there):
                    pltpu.make_async_remote_copy(
                        src_ref=send4.at[there],
                        dst_ref=recv4.at[mine],
                        send_sem=send_sem.at[stage],
                        recv_sem=recv_sem.at[2 + PAIR],
                        device_id=(me, there),
                        device_id_type=MESH,
                    ).start()

            @pl.when(jnp.logical_and(plane >= targets[0], plane <= targets[-1]))
            def _():
                whole(stage, send4, len(targets) - 1).wait_send()

            @pl.when(jnp.logical_or(plane < targets[0], plane > targets[-1]))
            def _():
                whole(stage, send4, len(targets)).wait_send()

        deliver(range(planes // 4), 2 + PAIR)
        deliver(range(planes // 4, planes // 2), 3 + PAIR)
        deliver(range(planes // 2, planes), 4 + PAIR)

    channel = lax.broadcasted_iota(jnp.int32, (channels, LANES), 0)
    loads[3].wait()
    loads[4].wait()
    skip = jnp.zeros((channels, LANES), jnp.float32)
    for c in range(channels):
        skip = jnp.where(channel == c, skip_scalars[c], skip)

    @pl.when(is_owner)
    def _():
        whole(2 + PAIR, recv4, owners - 1).wait_recv()

    @pl.when(jnp.logical_not(is_owner))
    def _():
        whole(2 + PAIR, recv4, owners).wait_recv()

    arrived = recv4[...].astype(jnp.float32)
    row = 0
    for owner in range(owners):
        rows = PAIR * ROWS if ahead <= owner < ahead + doubles else ROWS
        rows4[row : row + rows, :] = arrived[owner, :rows, :]
        row += rows
    for s in range(ROWS):
        columns = slice(s * LANES, (s + 1) * LANES)
        conv = rows4[pl.ds(s, channels, stride=ROWS), :]
        total = conv + skip * mixed[:, columns]
        out_ref[:, columns] = (outer[:, columns].astype(jnp.float32) * total).astype(jnp.bfloat16)

    @pl.when(is_owner)
    def _():
        whole(1, send2.at[0], blocks - 1).wait_send()
        whole(1 + PAIR, send3, blocks - 1).wait_send()

    @pl.when(is_single)
    def _():
        whole(0, send1, channels - 1).wait_send()

    @pl.when(is_double)
    def _():
        whole(0, send1, channels - PAIR).wait_send()
        whole(2, send2.at[1], blocks - 1).wait_send()

    @pl.when(jnp.logical_not(is_owner))
    def _():
        whole(0, send1, channels).wait_send()


def local(planes, blocks, outer_gate, inner_gate, signal, filter_taps, skip_gain):
    channels, tokens = signal.shape
    owners = sum(layout(planes))
    tables = make_tables(planes, blocks)
    bf16, f32 = jnp.bfloat16, jnp.float32
    scratch = [pltpu.VMEM((channels, tokens), bf16)] * 4
    scratch += [pltpu.SMEM((channels,), f32)]
    scratch += [pltpu.VMEM(t.shape, t.dtype) for t in tables]
    scratch += [
        pltpu.VMEM((channels, tokens), f32),
        pltpu.VMEM((channels * 2 * ROWS, LANES), f32),
        pltpu.VMEM((channels, 2 * ROWS, LANES), bf16),
        pltpu.VMEM((planes, PAIR, 2 * ROWS, LANES), bf16),
        pltpu.VMEM((PAIR, blocks, 2 * ROWS, LANES), bf16),
        pltpu.VMEM((PAIR, blocks, 2 * ROWS, LANES), bf16),
    ]
    scratch += [pltpu.VMEM((blocks, ROWS, LANES), f32)] * 4
    scratch += [
        pltpu.VMEM((blocks, PAIR * ROWS, LANES), f32),
        pltpu.VMEM((blocks, PAIR * ROWS, LANES), bf16),
        pltpu.VMEM((blocks, PAIR * ROWS, LANES), bf16),
        pltpu.VMEM((planes, PAIR * ROWS, LANES), bf16),
        pltpu.VMEM((owners, PAIR * ROWS, LANES), bf16),
        pltpu.VMEM((channels * ROWS, LANES), f32),
        pltpu.SemaphoreType.DMA((11,)),
        pltpu.SemaphoreType.DMA((5 + PAIR,)),
        pltpu.SemaphoreType.DMA((5 + PAIR,)),
    ]
    operands = (inner_gate, signal, filter_taps, outer_gate, skip_gain, *[jnp.asarray(t) for t in tables])
    return pl.pallas_call(
        functools.partial(kernel, planes, blocks),
        out_shape=pltpu.VMEM((channels, tokens), bf16),
        in_specs=[pl.BlockSpec(memory_space=pltpu.HBM)] * len(operands),
        out_specs=pl.BlockSpec(memory_space=pltpu.VMEM),
        scratch_shapes=scratch,
        compiler_params=pltpu.CompilerParams(
            collective_id=0, has_side_effects=True, vmem_limit_bytes=16 * 2**20
        ),
        name="hyena_conv",
    )(*[pltpu.with_memory_space_constraint(operand, pltpu.HBM) for operand in operands])


def solution(mesh):
    spec = P(None, ("ctx", "ch"))
    return jax.shard_map(
        functools.partial(local, mesh.shape["ch"], mesh.shape["ctx"]),
        mesh=mesh,
        in_specs=(spec, spec, spec, spec, P()),
        out_specs=spec,
        check_vma=False,
    )
```

```python
import functools
import math

import jax
import jax.numpy as jnp
import ml_dtypes
import numpy as np
from jax import lax
from jax.experimental import pallas as pl
from jax.experimental.pallas import tpu as pltpu
from jax.sharding import PartitionSpec as P

MESH = pl.DeviceIdType.MESH
LANES = 128
ROWS = 8
PAIR = 2


def split_bf16(table):
    high = table.astype(ml_dtypes.bfloat16)
    low = (table - high.astype(np.float64)).astype(ml_dtypes.bfloat16)
    return np.stack([high, low])


def make_tables(planes, blocks):
    units = ROWS * planes
    length = units * LANES
    part = units // blocks
    block, kind, row = np.meshgrid(np.arange(blocks), np.arange(2), np.arange(part), indexing="ij")
    row_first = (block * part + row).reshape(-1)
    row_kind = kind.reshape(-1)
    plane, column_kind, sub = np.meshgrid(np.arange(planes), np.arange(2), np.arange(ROWS), indexing="ij")
    unit = (plane * ROWS + sub).reshape(-1)
    column_kind = column_kind.reshape(-1)
    lane = np.arange(LANES)

    angle = 0.5 * np.pi * LANES * unit[None, :] / length
    angle = angle - 2 * np.pi * ((row_first[:, None] * unit[None, :]) % units) / units
    same = row_kind[:, None] == column_kind[None, :]
    first = np.concatenate([np.cos(angle) * same, np.sin(angle) * same])

    angle = 0.5 * np.pi * lane[None, :] / length - 2 * np.pi * row_first[:, None] * lane[None, :] / length
    twist = np.stack([np.cos(angle), np.sin(angle)])

    angle = 2 * np.pi * ((lane[:, None] * lane[None, :]) % LANES) / LANES
    cosine, sine = np.cos(angle), np.sin(angle)
    second = np.block([[cosine, -sine], [sine, cosine]])
    back = np.concatenate([cosine, sine], axis=1)

    real, imag = twist[0], -twist[1]
    is_real = row_kind[:, None] == 0
    untwist = np.stack([np.where(is_real, real, -imag), np.where(is_real, -imag, -real)])

    every_unit = np.arange(units)
    angle = -0.5 * np.pi * LANES * every_unit[:, None] / length
    angle = angle + 2 * np.pi * ((every_unit[:, None] * row_first[None, :]) % units) / units
    last = np.concatenate([np.cos(angle), -np.sin(angle)], axis=1) / length
    return (
        split_bf16(first),
        twist.astype(np.float32),
        split_bf16(second),
        back.astype(ml_dtypes.bfloat16),
        untwist.astype(np.float32),
        last.astype(ml_dtypes.bfloat16),
    )


def dot(left, right):
    return jnp.dot(left, right, preferred_element_type=jnp.float32)


def halves(value):
    high = value.astype(jnp.bfloat16)
    low = (value - high.astype(jnp.float32)).astype(jnp.bfloat16)
    return high, low


def away(k, size, ring):
    def around(k, n):
        return min(k, n - k)

    if ring:
        return around(k, size)
    side = max(1, math.isqrt(size // 2))
    return around(k // (2 * side), side) + around(k // 2 % side, side)


def far_first(size, ring):
    return sorted(range(1, size), key=lambda k: -away(k, size, ring))


def layout(planes):
    quarter = planes // 4
    return quarter, quarter, quarter


def wrap(position, size):
    return lax.rem(position, jnp.int32(size))


def kernel(planes, blocks, inner_hbm, signal_hbm, taps_hbm, outer_hbm, skip_hbm, first_hbm, twist_hbm,
           second_hbm, back_hbm, untwist_hbm, last_hbm, out_ref,
           inner, signal, taps, outer, skip_scalars, first, twist, second, back, untwist, last,
           mixed, staged, send1, recv1, send2, recv2, xa, xb, ha, hb, product, send3, recv3, send4, recv4, rows4,
           load_sem, send_sem, recv_sem):
    me = lax.axis_index("ctx")
    plane = lax.axis_index("ch")
    channels = planes
    ahead, doubles, behind = layout(planes)
    owners = ahead + doubles + behind


    def rank(z):
        return wrap(z + ahead, planes)

    def has_two(owner):
        return jnp.logical_and(owner >= ahead, owner < ahead + doubles)

    def has_one(owner):
        return jnp.logical_and(owner < owners, jnp.logical_not(has_two(owner)))

    def channel_of(owner):
        return owner + jnp.clip(owner - ahead, 0, doubles)

    units = ROWS * planes
    part = units // blocks
    is_owner = rank(plane) < owners
    mine = rank(plane)
    is_double = has_two(mine)
    is_single = has_one(mine)
    ring = far_first(planes, True)
    flat = far_first(blocks, False)

    barrier = pltpu.get_barrier_semaphore()

    sources = (inner_hbm, signal_hbm, taps_hbm, outer_hbm, skip_hbm, first_hbm, twist_hbm, second_hbm,
               back_hbm, untwist_hbm, last_hbm)
    places = (inner, signal, taps, outer, skip_scalars, first, twist, second, back, untwist, last)
    loads = [pltpu.make_async_copy(s, d, load_sem.at[i]) for i, (s, d) in enumerate(zip(sources, places))]
    for load in loads[:3]:
        load.start()

    @pl.when(is_owner)
    def _():
        for k in ring:
            pl.semaphore_signal(barrier, inc=1, device_id=(me, wrap(plane + k, planes)), device_id_type=MESH)
        for k in flat:
            pl.semaphore_signal(barrier, inc=1, device_id=(wrap(me + k, blocks), plane), device_id_type=MESH)

    for load in loads[3:5]:
        load.start()
    for load in loads[:3]:
        load.wait()

    gated = inner[...].astype(jnp.float32) * signal[...].astype(jnp.float32)
    gated = gated.astype(jnp.bfloat16).astype(jnp.float32)
    mixed[...] = gated
    filters = taps[...].astype(jnp.float32)
    for s in range(ROWS):
        columns = slice(s * LANES, (s + 1) * LANES)
        staged[pl.ds(s, channels, stride=2 * ROWS), :] = gated[:, columns]
        staged[pl.ds(ROWS + s, channels, stride=2 * ROWS), :] = filters[:, columns]
    send1[...] = staged[: channels * 2 * ROWS, :].reshape(channels, 2 * ROWS, LANES).astype(jnp.bfloat16)

    pl.semaphore_wait(barrier, jnp.where(is_owner, owners + blocks - 2, owners))

    def remote(stage, source, target, device):
        return pltpu.make_async_remote_copy(
            src_ref=source,
            dst_ref=target,
            send_sem=send_sem.at[stage],
            recv_sem=recv_sem.at[stage],
            device_id=device,
            device_id_type=MESH,
        )

    def whole(stage, buffer, slots):
        return remote(stage, buffer.at[pl.ds(0, slots)], buffer.at[pl.ds(0, slots)], (me, plane))

    for k in ring:
        there = wrap(plane + k, planes)

        @pl.when(has_one(rank(there)))
        def _(there=there):
            remote(0, send1.at[channel_of(rank(there))], recv1.at[plane, 0], (me, there)).start()

        @pl.when(has_two(rank(there)))
        def _(there=there):
            remote(0, send1.at[pl.ds(channel_of(rank(there)), PAIR)], recv1.at[plane], (me, there)).start()

    @pl.when(is_owner)
    def _():
        for load in loads[5:]:
            load.start()

        @pl.when(is_single)
        def _():
            recv1[plane, 0] = send1[channel_of(mine)]

        @pl.when(is_double)
        def _():
            recv1[plane] = send1[pl.ds(channel_of(mine), PAIR)]

        for load in loads[5:]:
            load.wait()

        @pl.when(is_single)
        def _():
            whole(0, recv1.at[:, 0], planes - 1).wait_recv()

        @pl.when(is_double)
        def _():
            whole(0, recv1, planes - 1).wait_recv()

        values = jnp.concatenate([recv1[:, c].reshape(2 * units, LANES) for c in range(PAIR)], axis=1)
        along = dot(first[0], values) + dot(first[1], values)
        def forward(c):
            real = along[: 2 * units, c * LANES : (c + 1) * LANES]
            imag = along[2 * units :, c * LANES : (c + 1) * LANES]
            turned = jnp.concatenate(
                [real * twist[0] - imag * twist[1], real * twist[1] + imag * twist[0]], axis=1
            )
            high, low = halves(turned)
            spectrum = dot(high, second[0]) + dot(low, second[0]) + dot(high, second[1])
            send2[c] = jnp.concatenate(
                [
                    spectrum[:, :LANES].reshape(blocks, ROWS, LANES),
                    spectrum[:, LANES:].reshape(blocks, ROWS, LANES),
                ],
                axis=1,
            ).astype(jnp.bfloat16)
            recv2[c, me] = send2[c, me]
            for k in flat:
                there = wrap(me + k, blocks)
                remote(1 + c, send2.at[c, there], recv2.at[c, me], (there, plane)).start()

        forward(0)
        pl.when(is_double)(functools.partial(forward, 1))

        upper = lax.broadcasted_iota(jnp.int32, (blocks, ROWS, LANES), 1) < part
        sign = jnp.where(lax.broadcasted_iota(jnp.int32, (ROWS, LANES), 0) < part, 1.0, -1.0)
        group = min(8, blocks)
        def multiply(c):
            whole(1 + c, recv2.at[c], blocks - 1).wait_recv()
            pieces = recv2[c].astype(jnp.float32)
            real, imag = pieces[:, :ROWS], pieces[:, ROWS:]
            real_rolled = jnp.roll(real, part, axis=1)
            imag_rolled = jnp.roll(imag, part, axis=1)
            xa[...] = jnp.where(upper, real, imag_rolled)
            xb[...] = jnp.where(upper, imag, real_rolled)
            ha[...] = jnp.where(upper, real_rolled, real)
            hb[...] = jnp.where(upper, -imag_rolled, imag)
            before = jnp.zeros((ROWS, LANES), jnp.float32)
            for start in range(0, blocks, group):
                sums = [jnp.zeros((ROWS, LANES), jnp.float32) for _ in range(group)]
                for i in range(start + group):
                    x_direct, x_crossed = xa[i], xb[i]
                    for offset in range(group):
                        j = start + offset - i
                        if j >= 0:
                            sums[offset] = sums[offset] + (x_direct * ha[j] + x_crossed * hb[j])
                for offset in range(group):
                    product[start + offset, c * ROWS : (c + 1) * ROWS, :] = sums[offset] + sign * jnp.roll(
                        before, part, axis=0
                    )
                    before = sums[offset]

        multiply(0)
        pl.when(is_double)(functools.partial(multiply, 1))

        @pl.when(is_single)
        def _():
            product[:, ROWS:, :] = jnp.zeros((blocks, ROWS, LANES), jnp.float32)

        send3[...] = product[...].astype(jnp.bfloat16)
        recv3[me] = send3[me]
        for there in sorted(range(blocks), key=lambda k: away(k, blocks, False)):

            @pl.when(there != me)
            def _(there=there):
                remote(1 + PAIR, send3.at[there], recv3.at[me], (there, plane)).start()
        whole(1 + PAIR, recv3, blocks - 1).wait_recv()

        waves = recv3[...].reshape(blocks * PAIR * ROWS, LANES)
        lanes_back = dot(waves, back[...]).reshape(blocks, PAIR, ROWS, 2 * LANES)
        turned = []
        for c in range(PAIR):
            lanes_c = lanes_back[:, c].reshape(2 * units, 2 * LANES)
            first_half, second_half = lanes_c[:, :LANES], lanes_c[:, LANES:]
            turned.append(
                jnp.concatenate(
                    [
                        first_half * untwist[0] + second_half * untwist[1],
                        second_half * untwist[0] - first_half * untwist[1],
                    ],
                    axis=0,
                )
            )
        result = dot(last[...], jnp.concatenate(turned, axis=1).astype(jnp.bfloat16))
        send4[...] = jnp.concatenate(
            [result[:, c * LANES : (c + 1) * LANES].reshape(planes, ROWS, LANES) for c in range(PAIR)], axis=1
        ).astype(jnp.bfloat16)
        recv4[mine] = send4[plane]
        for k in ring:
            there = wrap(plane + k, planes)
            if 1: continue
            remote(2 + PAIR, send4.at[there], recv4.at[mine], (me, there)).start()

        def deliver(targets, stage):
            for there in targets:

                @pl.when(there != plane)
                def _(there=there):
                    pltpu.make_async_remote_copy(
                        src_ref=send4.at[there],
                        dst_ref=recv4.at[mine],
                        send_sem=send_sem.at[stage],
                        recv_sem=recv_sem.at[2 + PAIR],
                        device_id=(me, there),
                        device_id_type=MESH,
                    ).start()

            @pl.when(jnp.logical_and(plane >= targets[0], plane <= targets[-1]))
            def _():
                whole(stage, send4, len(targets) - 1).wait_send()

            @pl.when(jnp.logical_or(plane < targets[0], plane > targets[-1]))
            def _():
                whole(stage, send4, len(targets)).wait_send()

        deliver(range(planes // 4), 2 + PAIR)
        deliver(range(planes // 4, planes // 2), 3 + PAIR)
        deliver(range(planes // 2, planes), 4 + PAIR)

    channel = lax.broadcasted_iota(jnp.int32, (channels, LANES), 0)
    loads[3].wait()
    loads[4].wait()
    skip = jnp.zeros((channels, LANES), jnp.float32)
    for c in range(channels):
        skip = jnp.where(channel == c, skip_scalars[c], skip)

    @pl.when(is_owner)
    def _():
        whole(2 + PAIR, recv4, owners - 1).wait_recv()

    @pl.when(jnp.logical_not(is_owner))
    def _():
        whole(2 + PAIR, recv4, owners).wait_recv()

    arrived = recv4[...].astype(jnp.float32)
    row = 0
    for owner in range(owners):
        rows = PAIR * ROWS if ahead <= owner < ahead + doubles else ROWS
        rows4[row : row + rows, :] = arrived[owner, :rows, :]
        row += rows
    for s in range(ROWS):
        columns = slice(s * LANES, (s + 1) * LANES)
        conv = rows4[pl.ds(s, channels, stride=ROWS), :]
        total = conv + skip * mixed[:, columns]
        out_ref[:, columns] = (outer[:, columns].astype(jnp.float32) * total).astype(jnp.bfloat16)

    @pl.when(is_owner)
    def _():
        whole(1, send2.at[0], blocks - 1).wait_send()
        whole(1 + PAIR, send3, blocks - 1).wait_send()

    @pl.when(is_single)
    def _():
        whole(0, send1, channels - 1).wait_send()

    @pl.when(is_double)
    def _():
        whole(0, send1, channels - PAIR).wait_send()
        whole(2, send2.at[1], blocks - 1).wait_send()

    @pl.when(jnp.logical_not(is_owner))
    def _():
        whole(0, send1, channels).wait_send()


def local(planes, blocks, outer_gate, inner_gate, signal, filter_taps, skip_gain):
    channels, tokens = signal.shape
    owners = sum(layout(planes))
    tables = make_tables(planes, blocks)
    bf16, f32 = jnp.bfloat16, jnp.float32
    scratch = [pltpu.VMEM((channels, tokens), bf16)] * 4
    scratch += [pltpu.SMEM((channels,), f32)]
    scratch += [pltpu.VMEM(t.shape, t.dtype) for t in tables]
    scratch += [
        pltpu.VMEM((channels, tokens), f32),
        pltpu.VMEM(((channels + 1) * 2 * ROWS, LANES), f32),
        pltpu.VMEM((channels, 2 * ROWS, LANES), bf16),
        pltpu.VMEM((planes, PAIR, 2 * ROWS, LANES), bf16),
        pltpu.VMEM((PAIR, blocks, 2 * ROWS, LANES), bf16),
        pltpu.VMEM((PAIR, blocks, 2 * ROWS, LANES), bf16),
    ]
    scratch += [pltpu.VMEM((blocks, ROWS, LANES), f32)] * 4
    scratch += [
        pltpu.VMEM((blocks, PAIR * ROWS, LANES), f32),
        pltpu.VMEM((blocks, PAIR * ROWS, LANES), bf16),
        pltpu.VMEM((blocks, PAIR * ROWS, LANES), bf16),
        pltpu.VMEM((planes, PAIR * ROWS, LANES), bf16),
        pltpu.VMEM((owners, PAIR * ROWS, LANES), bf16),
        pltpu.VMEM(((channels + 1) * ROWS, LANES), f32),
        pltpu.SemaphoreType.DMA((11,)),
        pltpu.SemaphoreType.DMA((5 + PAIR,)),
        pltpu.SemaphoreType.DMA((5 + PAIR,)),
    ]
    operands = (inner_gate, signal, filter_taps, outer_gate, skip_gain, *[jnp.asarray(t) for t in tables])
    return pl.pallas_call(
        functools.partial(kernel, planes, blocks),
        out_shape=pltpu.VMEM((channels, tokens), bf16),
        in_specs=[pl.BlockSpec(memory_space=pltpu.HBM)] * len(operands),
        out_specs=pl.BlockSpec(memory_space=pltpu.VMEM),
        scratch_shapes=scratch,
        compiler_params=pltpu.CompilerParams(
            collective_id=0, has_side_effects=True, vmem_limit_bytes=16 * 2**20
        ),
        name="hyena_conv",
    )(*[pltpu.with_memory_space_constraint(operand, pltpu.HBM) for operand in operands])


def solution(mesh):
    spec = P(None, ("ctx", "ch"))
    return jax.shard_map(
        functools.partial(local, mesh.shape["ch"], mesh.shape["ctx"]),
        mesh=mesh,
        in_specs=(spec, spec, spec, spec, P()),
        out_specs=spec,
        check_vma=False,
    )
```

```python
import functools
import math

import jax
import jax.numpy as jnp
import ml_dtypes
import numpy as np
from jax import lax
from jax.experimental import pallas as pl
from jax.experimental.pallas import tpu as pltpu
from jax.sharding import PartitionSpec as P

MESH = pl.DeviceIdType.MESH
LANES = 128
ROWS = 8
PAIR = 2


def split_bf16(table):
    high = table.astype(ml_dtypes.bfloat16)
    low = (table - high.astype(np.float64)).astype(ml_dtypes.bfloat16)
    return np.stack([high, low])


def make_tables(planes, blocks):
    units = ROWS * planes
    length = units * LANES
    part = units // blocks
    block, kind, row = np.meshgrid(np.arange(blocks), np.arange(2), np.arange(part), indexing="ij")
    row_first = (block * part + row).reshape(-1)
    row_kind = kind.reshape(-1)
    plane, column_kind, sub = np.meshgrid(np.arange(planes), np.arange(2), np.arange(ROWS), indexing="ij")
    unit = (plane * ROWS + sub).reshape(-1)
    column_kind = column_kind.reshape(-1)
    lane = np.arange(LANES)

    angle = 0.5 * np.pi * LANES * unit[None, :] / length
    angle = angle - 2 * np.pi * ((row_first[:, None] * unit[None, :]) % units) / units
    same = row_kind[:, None] == column_kind[None, :]
    first = np.concatenate([np.cos(angle) * same, np.sin(angle) * same])

    angle = 0.5 * np.pi * lane[None, :] / length - 2 * np.pi * row_first[:, None] * lane[None, :] / length
    twist = np.stack([np.cos(angle), np.sin(angle)])

    angle = 2 * np.pi * ((lane[:, None] * lane[None, :]) % LANES) / LANES
    cosine, sine = np.cos(angle), np.sin(angle)
    second = np.block([[cosine, -sine], [sine, cosine]])
    back = np.concatenate([cosine, sine], axis=1)

    real, imag = twist[0], -twist[1]
    is_real = row_kind[:, None] == 0
    untwist = np.stack([np.where(is_real, real, -imag), np.where(is_real, -imag, -real)])

    every_unit = np.arange(units)
    angle = -0.5 * np.pi * LANES * every_unit[:, None] / length
    angle = angle + 2 * np.pi * ((every_unit[:, None] * row_first[None, :]) % units) / units
    last = np.concatenate([np.cos(angle), -np.sin(angle)], axis=1) / length
    return (
        split_bf16(first),
        twist.astype(np.float32),
        split_bf16(second),
        back.astype(ml_dtypes.bfloat16),
        untwist.astype(np.float32),
        last.astype(ml_dtypes.bfloat16),
    )


def dot(left, right):
    return jnp.dot(left, right, preferred_element_type=jnp.float32)


def halves(value):
    high = value.astype(jnp.bfloat16)
    low = (value - high.astype(jnp.float32)).astype(jnp.bfloat16)
    return high, low


def away(k, size, ring):
    def around(k, n):
        return min(k, n - k)

    if ring:
        return around(k, size)
    side = max(1, math.isqrt(size // 2))
    return around(k // (2 * side), side) + around(k // 2 % side, side)


def far_first(size, ring):
    return sorted(range(1, size), key=lambda k: -away(k, size, ring))


def layout(planes):
    quarter = planes // 4
    return quarter, quarter, quarter


def wrap(position, size):
    return lax.rem(position, jnp.int32(size))


def kernel(planes, blocks, inner_hbm, signal_hbm, taps_hbm, outer_hbm, skip_hbm, first_hbm, twist_hbm,
           second_hbm, back_hbm, untwist_hbm, last_hbm, out_ref,
           inner, signal, taps, outer, skip_scalars, first, twist, second, back, untwist, last,
           mixed, staged, send1, recv1, send2, recv2, xa, xb, ha, hb, product, send3, recv3, send4, recv4, rows4,
           load_sem, send_sem, recv_sem):
    me = lax.axis_index("ctx")
    plane = lax.axis_index("ch")
    channels = planes
    ahead, doubles, behind = layout(planes)
    owners = ahead + doubles + behind


    def rank(z):
        return wrap(z + ahead, planes)

    def has_two(owner):
        return jnp.logical_and(owner >= ahead, owner < ahead + doubles)

    def has_one(owner):
        return jnp.logical_and(owner < owners, jnp.logical_not(has_two(owner)))

    def channel_of(owner):
        return owner + jnp.clip(owner - ahead, 0, doubles)

    units = ROWS * planes
    part = units // blocks
    is_owner = rank(plane) < owners
    mine = rank(plane)
    is_double = has_two(mine)
    is_single = has_one(mine)
    ring = far_first(planes, True)
    flat = far_first(blocks, False)

    barrier = pltpu.get_barrier_semaphore()

    sources = (inner_hbm, signal_hbm, taps_hbm, outer_hbm, skip_hbm, first_hbm, twist_hbm, second_hbm,
               back_hbm, untwist_hbm, last_hbm)
    places = (inner, signal, taps, outer, skip_scalars, first, twist, second, back, untwist, last)
    loads = [pltpu.make_async_copy(s, d, load_sem.at[i]) for i, (s, d) in enumerate(zip(sources, places))]
    for load in loads[:3]:
        load.start()

    @pl.when(is_owner)
    def _():
        for k in ring:
            pl.semaphore_signal(barrier, inc=1, device_id=(me, wrap(plane + k, planes)), device_id_type=MESH)
        for k in flat:
            pl.semaphore_signal(barrier, inc=1, device_id=(wrap(me + k, blocks), plane), device_id_type=MESH)

    for load in loads[3:5]:
        load.start()
    for load in loads[:3]:
        load.wait()

    gated = inner[...].astype(jnp.float32) * signal[...].astype(jnp.float32)
    gated = gated.astype(jnp.bfloat16).astype(jnp.float32)
    mixed[...] = gated
    filters = taps[...].astype(jnp.float32)
    for s in range(ROWS):
        columns = slice(s * LANES, (s + 1) * LANES)
        staged[pl.ds(s, channels, stride=2 * ROWS), :] = gated[:, columns]
        staged[pl.ds(ROWS + s, channels, stride=2 * ROWS), :] = filters[:, columns]
    send1[...] = staged[: channels * 2 * ROWS, :].reshape(channels, 2 * ROWS, LANES).astype(jnp.bfloat16)

    pl.semaphore_wait(barrier, jnp.where(is_owner, owners + blocks - 2, owners))

    def remote(stage, source, target, device):
        return pltpu.make_async_remote_copy(
            src_ref=source,
            dst_ref=target,
            send_sem=send_sem.at[stage],
            recv_sem=recv_sem.at[stage],
            device_id=device,
            device_id_type=MESH,
        )

    def whole(stage, buffer, slots):
        return remote(stage, buffer.at[pl.ds(0, slots)], buffer.at[pl.ds(0, slots)], (me, plane))

    def offer(k, two):
        there = wrap(plane + k, planes)

        @pl.when(has_two(rank(there)) if two else has_one(rank(there)))
        def _():
            if two:
                remote(0, send1.at[pl.ds(channel_of(rank(there)), PAIR)], recv1.at[plane], (me, there)).start()
            else:
                remote(0, send1.at[channel_of(rank(there))], recv1.at[plane, 0], (me, there)).start()

    order = [(k, two) for k in ring for two in (False, True)]
    for k, two in sorted(order, key=lambda item: -away(item[0], planes, True) - 0.5 * item[1]):
        offer(k, two)

    @pl.when(is_owner)
    def _():
        for load in loads[5:]:
            load.start()

        @pl.when(is_single)
        def _():
            recv1[plane, 0] = send1[channel_of(mine)]

        @pl.when(is_double)
        def _():
            recv1[plane] = send1[pl.ds(channel_of(mine), PAIR)]

        for load in loads[5:]:
            load.wait()

        @pl.when(is_single)
        def _():
            whole(0, recv1.at[:, 0], planes - 1).wait_recv()

        @pl.when(is_double)
        def _():
            whole(0, recv1, planes - 1).wait_recv()

        values = jnp.concatenate([recv1[:, c].reshape(2 * units, LANES) for c in range(PAIR)], axis=1)
        along = dot(first[0], values) + dot(first[1], values)
        def forward(c):
            real = along[: 2 * units, c * LANES : (c + 1) * LANES]
            imag = along[2 * units :, c * LANES : (c + 1) * LANES]
            turned = jnp.concatenate(
                [real * twist[0] - imag * twist[1], real * twist[1] + imag * twist[0]], axis=1
            )
            high, low = halves(turned)
            spectrum = dot(high, second[0]) + dot(low, second[0]) + dot(high, second[1])
            send2[c] = jnp.concatenate(
                [
                    spectrum[:, :LANES].reshape(blocks, ROWS, LANES),
                    spectrum[:, LANES:].reshape(blocks, ROWS, LANES),
                ],
                axis=1,
            ).astype(jnp.bfloat16)
            for k in flat:
                there = wrap(me + k, blocks)
                remote(1 + c, send2.at[c, there], recv2.at[c, me], (there, plane)).start()
            recv2[c, me] = send2[c, me]

        forward(0)
        pl.when(is_double)(functools.partial(forward, 1))

        upper = lax.broadcasted_iota(jnp.int32, (blocks, ROWS, LANES), 1) < part
        sign = jnp.where(lax.broadcasted_iota(jnp.int32, (ROWS, LANES), 0) < part, 1.0, -1.0)
        group = min(8, blocks)
        def multiply(c):
            whole(1 + c, recv2.at[c], blocks - 1).wait_recv()
            pieces = recv2[c].astype(jnp.float32)
            real, imag = pieces[:, :ROWS], pieces[:, ROWS:]
            real_rolled = jnp.roll(real, part, axis=1)
            imag_rolled = jnp.roll(imag, part, axis=1)
            xa[...] = jnp.where(upper, real, imag_rolled)
            xb[...] = jnp.where(upper, imag, real_rolled)
            ha[...] = jnp.where(upper, real_rolled, real)
            hb[...] = jnp.where(upper, -imag_rolled, imag)
            before = jnp.zeros((ROWS, LANES), jnp.float32)
            for start in range(0, blocks, group):
                sums = [jnp.zeros((ROWS, LANES), jnp.float32) for _ in range(group)]
                for i in range(start + group):
                    x_direct, x_crossed = xa[i], xb[i]
                    for offset in range(group):
                        j = start + offset - i
                        if j >= 0:
                            sums[offset] = sums[offset] + (x_direct * ha[j] + x_crossed * hb[j])
                for offset in range(group):
                    product[start + offset, c * ROWS : (c + 1) * ROWS, :] = sums[offset] + sign * jnp.roll(
                        before, part, axis=0
                    )
                    before = sums[offset]

        multiply(0)
        pl.when(is_double)(functools.partial(multiply, 1))

        @pl.when(is_single)
        def _():
            product[:, ROWS:, :] = jnp.zeros((blocks, ROWS, LANES), jnp.float32)

        send3[...] = product[...].astype(jnp.bfloat16)
        for there in sorted(range(blocks), key=lambda k: away(k, blocks, False)):

            @pl.when(there != me)
            def _(there=there):
                remote(1 + PAIR, send3.at[there], recv3.at[me], (there, plane)).start()
        recv3[me] = send3[me]
        whole(1 + PAIR, recv3, blocks - 1).wait_recv()

        waves = recv3[...].reshape(blocks * PAIR * ROWS, LANES)
        lanes_back = dot(waves, back[...]).reshape(blocks, PAIR, ROWS, 2 * LANES)
        turned = []
        for c in range(PAIR):
            lanes_c = lanes_back[:, c].reshape(2 * units, 2 * LANES)
            first_half, second_half = lanes_c[:, :LANES], lanes_c[:, LANES:]
            turned.append(
                jnp.concatenate(
                    [
                        first_half * untwist[0] + second_half * untwist[1],
                        second_half * untwist[0] - first_half * untwist[1],
                    ],
                    axis=0,
                )
            )
        result = dot(last[...], jnp.concatenate(turned, axis=1).astype(jnp.bfloat16))
        send4[...] = jnp.concatenate(
            [result[:, c * LANES : (c + 1) * LANES].reshape(planes, ROWS, LANES) for c in range(PAIR)], axis=1
        ).astype(jnp.bfloat16)
        recv4[mine] = send4[plane]
        for k in ring:
            there = wrap(plane + k, planes)
            if 1: continue
            remote(2 + PAIR, send4.at[there], recv4.at[mine], (me, there)).start()

        def deliver(targets, stage):
            for there in targets:

                @pl.when(there != plane)
                def _(there=there):
                    pltpu.make_async_remote_copy(
                        src_ref=send4.at[there],
                        dst_ref=recv4.at[mine],
                        send_sem=send_sem.at[stage],
                        recv_sem=recv_sem.at[2 + PAIR],
                        device_id=(me, there),
                        device_id_type=MESH,
                    ).start()

            @pl.when(jnp.logical_and(plane >= targets[0], plane <= targets[-1]))
            def _():
                whole(stage, send4, len(targets) - 1).wait_send()

            @pl.when(jnp.logical_or(plane < targets[0], plane > targets[-1]))
            def _():
                whole(stage, send4, len(targets)).wait_send()

        deliver(range(planes // 4), 2 + PAIR)
        deliver(range(planes // 4, planes // 2), 3 + PAIR)
        deliver(range(planes // 2, planes), 4 + PAIR)

    channel = lax.broadcasted_iota(jnp.int32, (channels, LANES), 0)
    loads[3].wait()
    loads[4].wait()
    skip = jnp.zeros((channels, LANES), jnp.float32)
    for c in range(channels):
        skip = jnp.where(channel == c, skip_scalars[c], skip)

    @pl.when(is_owner)
    def _():
        whole(2 + PAIR, recv4, owners - 1).wait_recv()

    @pl.when(jnp.logical_not(is_owner))
    def _():
        whole(2 + PAIR, recv4, owners).wait_recv()

    arrived = recv4[...].astype(jnp.float32)
    row = 0
    for owner in range(owners):
        rows = PAIR * ROWS if ahead <= owner < ahead + doubles else ROWS
        rows4[row : row + rows, :] = arrived[owner, :rows, :]
        row += rows
    for s in range(ROWS):
        columns = slice(s * LANES, (s + 1) * LANES)
        conv = rows4[pl.ds(s, channels, stride=ROWS), :]
        total = conv + skip * mixed[:, columns]
        out_ref[:, columns] = (outer[:, columns].astype(jnp.float32) * total).astype(jnp.bfloat16)

    @pl.when(is_owner)
    def _():
        whole(1, send2.at[0], blocks - 1).wait_send()
        whole(1 + PAIR, send3, blocks - 1).wait_send()

    @pl.when(is_single)
    def _():
        whole(0, send1, channels - 1).wait_send()

    @pl.when(is_double)
    def _():
        whole(0, send1, channels - PAIR).wait_send()
        whole(2, send2.at[1], blocks - 1).wait_send()

    @pl.when(jnp.logical_not(is_owner))
    def _():
        whole(0, send1, channels).wait_send()


def local(planes, blocks, outer_gate, inner_gate, signal, filter_taps, skip_gain):
    channels, tokens = signal.shape
    owners = sum(layout(planes))
    tables = make_tables(planes, blocks)
    bf16, f32 = jnp.bfloat16, jnp.float32
    scratch = [pltpu.VMEM((channels, tokens), bf16)] * 4
    scratch += [pltpu.SMEM((channels,), f32)]
    scratch += [pltpu.VMEM(t.shape, t.dtype) for t in tables]
    scratch += [
        pltpu.VMEM((channels, tokens), f32),
        pltpu.VMEM(((channels + 1) * 2 * ROWS, LANES), f32),
        pltpu.VMEM((channels, 2 * ROWS, LANES), bf16),
        pltpu.VMEM((planes, PAIR, 2 * ROWS, LANES), bf16),
        pltpu.VMEM((PAIR, blocks, 2 * ROWS, LANES), bf16),
        pltpu.VMEM((PAIR, blocks, 2 * ROWS, LANES), bf16),
    ]
    scratch += [pltpu.VMEM((blocks, ROWS, LANES), f32)] * 4
    scratch += [
        pltpu.VMEM((blocks, PAIR * ROWS, LANES), f32),
        pltpu.VMEM((blocks, PAIR * ROWS, LANES), bf16),
        pltpu.VMEM((blocks, PAIR * ROWS, LANES), bf16),
        pltpu.VMEM((planes, PAIR * ROWS, LANES), bf16),
        pltpu.VMEM((owners, PAIR * ROWS, LANES), bf16),
        pltpu.VMEM(((channels + 1) * ROWS, LANES), f32),
        pltpu.SemaphoreType.DMA((11,)),
        pltpu.SemaphoreType.DMA((5 + PAIR,)),
        pltpu.SemaphoreType.DMA((5 + PAIR,)),
    ]
    operands = (inner_gate, signal, filter_taps, outer_gate, skip_gain, *[jnp.asarray(t) for t in tables])
    return pl.pallas_call(
        functools.partial(kernel, planes, blocks),
        out_shape=pltpu.VMEM((channels, tokens), bf16),
        in_specs=[pl.BlockSpec(memory_space=pltpu.HBM)] * len(operands),
        out_specs=pl.BlockSpec(memory_space=pltpu.VMEM),
        scratch_shapes=scratch,
        compiler_params=pltpu.CompilerParams(
            collective_id=0, has_side_effects=True, vmem_limit_bytes=16 * 2**20
        ),
        name="hyena_conv",
    )(*[pltpu.with_memory_space_constraint(operand, pltpu.HBM) for operand in operands])


def solution(mesh):
    spec = P(None, ("ctx", "ch"))
    return jax.shard_map(
        functools.partial(local, mesh.shape["ch"], mesh.shape["ctx"]),
        mesh=mesh,
        in_specs=(spec, spec, spec, spec, P()),
        out_specs=spec,
        check_vma=False,
    )
```
